32 devices in a mesh: groups: 2 (over y), seq: 16 (over z, x, core).
Axes of the slice: x: 2, y: 2, z: 4, core: 2. Of those that a mesh axis runs over, the one named last changes fastest.
Arguments:
- visible_tokens: bfloat16 [1024, 1280], P(('groups', 'seq')), parts along dimension 0, may hold values from -6 to 6
- restore_order: int32 [4096], P(('groups', 'seq')), parts along dimension 0, may hold values from 0 to 2047, as said below
- encoder_project: bfloat16 [1280, 1920], replicated, may hold values from -6 to 6
- encoder_output: bfloat16 [640, 1280], replicated, may hold values from -0.25 to 0.25
- decoder_embed: bfloat16 [1280, 512], replicated, may hold values from -0.15625 to 0.15625
- mask_token: bfloat16 [512], replicated, may hold values from -1.5 to 1.5
- position_table: bfloat16 [2048, 512], P('seq'), may hold values from -4.5 to 4.5
- decoder_project: bfloat16 [512, 768], replicated, may hold values from -6 to 6
- decoder_output: bfloat16 [256, 512], replicated, may hold values from -0.375 to 0.375
- expand_weight: bfloat16 [512, 2048], replicated, may hold values from -0.25 to 0.25
- shrink_weight: bfloat16 [2048, 512], replicated, may hold values from -0.125 to 0.125
Outputs:
- latent: bfloat16 [1024, 1280], P(('groups', 'seq')), parts along dimension 0
- decoded: bfloat16 [4096, 512], P(('groups', 'seq')), parts along dimension 0
The draws below stay inside these ranges and needn't reach their ends.
There are 2 independent parts, one for each index of `groups`. The reference program is written for one: setup_inputs(seed, part) draws one part's arguments, and reference() takes and returns one part's arrays. A program takes and returns all parts, laid end to end along the dimension named above; an argument that names none is the same for every part. Nothing has to cross between parts.
Inputs may be any that keep to these rules, and one draw needn't show every extreme that they name: `restore_order`: a permutation of the patch numbers; every device's 128 patches hold exactly 32 ranks under 512, and of the ranks r with the same r // 32, a device's patches hold either none or exactly 2.
All inputs are finite; a program needn't handle non-finite values.
Results may differ from the reference program's by a relative error of at most 0.0095.
Values may be sent and summed in bfloat16 or wider, within the bound.
A program may use at most 128 MiB of HBM per device.

```python
import jax
import jax.numpy as jnp
from jax import lax

D = 1280
EH = 8
EDH = 80
DD = 512
DH = 8
DDH = 32
FFD = 2048
POS_DEV = 128
VIS_DEV = 32
NP = 2048
NVIS = 512


def draw_encoder_project(key, part):
    key = jax.random.fold_in(key, 11)
    first_key = jax.random.fold_in(key, 0)
    weights = jax.random.truncated_normal(first_key, -4.0, 4.0, (D, 3 * EH * EDH), jnp.float32) * D ** (-0.5)
    return jnp.clip(weights, -6.0, 6.0).astype(jnp.bfloat16)


def draw_decoder_project(key, part):
    key = jax.random.fold_in(key, 23)
    first_key = jax.random.fold_in(key, 0)
    weights = jax.random.truncated_normal(first_key, -4.0, 4.0, (DD, 3 * DH * DDH), jnp.float32) * DD ** (-0.5)
    return jnp.clip(weights, -6.0, 6.0).astype(jnp.bfloat16)


def draw_position_table(key, part):
    key = jax.random.fold_in(key, 41)
    entries = jax.random.truncated_normal(key, -3.0, 3.0, (NP, DD), jnp.float32) * 1.5
    return jnp.clip(entries, -4.5, 4.5).astype(jnp.bfloat16)


def draw_restore_order(key, part):
    key = jax.random.fold_in(key, 37)
    offset_key, shuffle_key, masked_key, place_key = jax.random.split(key, 4)
    devices = NP // POS_DEV
    span = min(VIS_DEV, devices)
    masked_dev = POS_DEV - VIS_DEV
    offsets = jax.random.permutation(offset_key, devices)[:span].astype(jnp.int32)
    shuffle = jax.random.permutation(shuffle_key, devices).astype(jnp.int32)
    inverse = jnp.zeros((devices,), jnp.int32).at[shuffle].set(jnp.arange(devices, dtype=jnp.int32))
    slots = jnp.arange(VIS_DEV, dtype=jnp.int32)
    column = slots % span
    level = slots // span
    device_ids = jnp.arange(devices, dtype=jnp.int32)[:, None]
    owners = inverse[(device_ids - offsets[column][None, :]) % devices]
    visible = owners * VIS_DEV + (column + level * span)[None, :]
    masked = (NVIS + jax.random.permutation(masked_key, NP - NVIS).astype(jnp.int32)).reshape(devices, masked_dev)
    contents = jnp.concatenate([visible, masked], axis=1).astype(jnp.int32)
    place_keys = jax.random.split(place_key, devices)
    places = jax.vmap(lambda one_key: jax.random.permutation(one_key, POS_DEV).astype(jnp.int32))(place_keys)
    rows = jax.vmap(lambda place, content: jnp.zeros((POS_DEV,), jnp.int32).at[place].set(content))(places, contents)
    return rows.reshape(NP).astype(jnp.int32)


def block_scale(stream_key, shape, pieces, least, high):
    level = 1.0
    for dim, shards_of in pieces:
        draws = jax.random.uniform(jax.random.fold_in(jax.random.fold_in(stream_key, 6), dim), (shards_of,), jnp.float32, least / len(pieces), high / len(pieces))
        level = level * jnp.repeat(jnp.exp(draws), shape[dim] // shards_of).reshape((-1,) + (1,) * (len(shape) - 1 - dim))
    return level


def bell_draw(own_key, dims, scale, limit, cuts=(), kind=jnp.bfloat16):
    values = scale * jax.random.normal(own_key, dims, jnp.float32)
    if cuts:
        values = values * block_scale(own_key, dims, cuts, -0.22, 0.18)
    return jnp.clip(values, -limit, limit).astype(kind)


def setup_inputs(seed: int = 0, part: int = 0) -> dict:
    key_list = jax.random.split(jax.random.key(seed), 12)
    part_keys = jax.random.split(jax.random.fold_in(key_list[11], part), 12)
    visible_tokens = bell_draw(part_keys[0], (NVIS, D), 1.0, 6.0, ((0, 16),))
    restore_order = draw_restore_order(jax.random.fold_in(jax.random.fold_in(key_list[11], part), 71), part)
    encoder_project = draw_encoder_project(jax.random.fold_in(key_list[11], 71), part)
    encoder_output = bell_draw(key_list[3], (EH * EDH, D), (EH * EDH) ** -0.5, 0.25)
    decoder_embed = bell_draw(key_list[4], (D, DD), D ** -0.5, 0.15625)
    mask_token = bell_draw(key_list[5], (DD,), 0.3, 1.5)
    position_table = draw_position_table(jax.random.fold_in(key_list[11], 71), part)
    decoder_project = draw_decoder_project(jax.random.fold_in(key_list[11], 71), part)
    decoder_output = bell_draw(key_list[8], (DH * DDH, DD), (DH * DDH) ** -0.5, 0.375)
    expand_weight = bell_draw(key_list[9], (DD, FFD), DD ** -0.5, 0.25)
    shrink_weight = bell_draw(key_list[10], (FFD, DD), FFD ** -0.5, 0.125)
    return {"visible_tokens": visible_tokens, "restore_order": restore_order, "encoder_project": encoder_project, "encoder_output": encoder_output, "decoder_embed": decoder_embed, "mask_token": mask_token, "position_table": position_table, "decoder_project": decoder_project, "decoder_output": decoder_output, "expand_weight": expand_weight, "shrink_weight": shrink_weight}


def normalize(values):
    values = values.astype(jnp.float32)
    centre = values - lax.optimization_barrier(jnp.mean(values, -1, keepdims=True))
    spread = lax.optimization_barrier(jnp.mean(centre * centre, -1, keepdims=True))
    return (centre * lax.rsqrt(spread + 1e-06)).astype(jnp.bfloat16)

def attend(queries, keys, values, heads):
    total, width = queries.shape
    size = width // heads
    block = min(512, total)
    blocks = total // block
    key_heads = keys.astype(jnp.float32).reshape(keys.shape[0], heads, size)
    value_heads = values.astype(jnp.float32).reshape(values.shape[0], heads, size)
    query_blocks = queries.astype(jnp.float32).reshape(blocks, block, heads, size)

    def one_block(query_block):
        scores = jnp.einsum('qhd,khd->hqk', query_block, key_heads) * size ** (-0.5)
        highest = lax.optimization_barrier(jnp.max(scores, -1, keepdims=True))
        powers = jnp.exp(scores - highest)
        weights = (powers / lax.optimization_barrier(jnp.sum(powers, -1, keepdims=True))).astype(jnp.bfloat16)
        result = jnp.einsum('hqk,khd->qhd', weights.astype(jnp.float32), value_heads)
        return result.reshape(block, width).astype(jnp.bfloat16)
    return lax.map(one_block, query_blocks).reshape(total, width)

def reference(visible_tokens, restore_order, encoder_project, encoder_output, decoder_embed, mask_token, position_table, decoder_project, decoder_output, expand_weight, shrink_weight):
    enc_width = encoder_output.shape[0]
    dec_width = decoder_output.shape[0]
    enc_act = jnp.dot(normalize(visible_tokens), encoder_project, preferred_element_type=jnp.float32).astype(jnp.bfloat16)
    enc_mix = attend(enc_act[:, :enc_width], enc_act[:, enc_width:2 * enc_width], enc_act[:, 2 * enc_width:], EH)
    latent = (visible_tokens.astype(jnp.float32) + jnp.dot(enc_mix, encoder_output, preferred_element_type=jnp.float32)).astype(jnp.bfloat16)
    embedded = jnp.dot(normalize(latent), decoder_embed, preferred_element_type=jnp.float32).astype(jnp.bfloat16)
    visible_count = latent.shape[0]
    chosen = jnp.minimum(restore_order, visible_count - 1).astype(jnp.int32)
    picked = jnp.take(embedded, chosen, axis=0).astype(jnp.float32)
    filled = jnp.where((restore_order < visible_count)[:, None], picked, mask_token.astype(jnp.float32)[None, :])
    dec_in = (filled + position_table.astype(jnp.float32)).astype(jnp.bfloat16)
    dec_act = jnp.dot(normalize(dec_in), decoder_project, preferred_element_type=jnp.float32).astype(jnp.bfloat16)
    dec_mix = attend(dec_act[:, :dec_width], dec_act[:, dec_width:2 * dec_width], dec_act[:, 2 * dec_width:], DH)
    middle = (dec_in.astype(jnp.float32) + jnp.dot(dec_mix, decoder_output, preferred_element_type=jnp.float32)).astype(jnp.bfloat16)
    hidden = jax.nn.gelu(jnp.dot(normalize(middle), expand_weight, preferred_element_type=jnp.float32), approximate=False).astype(jnp.bfloat16)
    decoded = (middle.astype(jnp.float32) + jnp.dot(hidden, shrink_weight, preferred_element_type=jnp.float32)).astype(jnp.bfloat16)
    return (latent, decoded)
```

```python
import functools

import jax
import jax.numpy as jnp
from jax import lax
from jax.experimental import pallas as pl
from jax.experimental.pallas import tpu as pltpu
from jax.sharding import PartitionSpec as P

EH = 8
DH = 8


def normalize(values):
    values = values.astype(jnp.float32)
    centre = values - jnp.mean(values, -1, keepdims=True)
    spread = jnp.mean(centre * centre, -1, keepdims=True)
    return (centre * lax.rsqrt(spread + 1e-06)).astype(jnp.bfloat16)


def attend(queries, keys, values, heads):
    total, width = queries.shape
    size = width // heads
    query_heads = queries.reshape(total, heads, size).transpose(1, 0, 2)
    key_heads = keys.reshape(keys.shape[0], heads, size).transpose(1, 0, 2)
    value_heads = values.reshape(values.shape[0], heads, size).transpose(1, 0, 2)

    def one_head(operands):
        query_part, key_part, value_part = operands
        scores = lax.dot_general(
            query_part, key_part, (((1,), (1,)), ((), ())), preferred_element_type=jnp.float32
        ) * size ** (-0.5)
        highest = jnp.max(scores, -1, keepdims=True)
        powers = jnp.exp(scores - highest)
        weights = (powers / jnp.sum(powers, -1, keepdims=True)).astype(jnp.bfloat16)
        return jnp.dot(weights, value_part, preferred_element_type=jnp.float32).astype(jnp.bfloat16)

    result = lax.map(one_head, (query_heads, key_heads, value_heads))
    return result.transpose(1, 0, 2).reshape(total, width)


def on_device_plain(
    visible_tokens,
    restore_order,
    encoder_project,
    encoder_output,
    decoder_embed,
    mask_token,
    position_table,
    decoder_project,
    decoder_output,
    expand_weight,
    shrink_weight,
):
    enc_width = encoder_output.shape[0]
    dec_width = decoder_output.shape[0]
    enc_act = jnp.dot(
        normalize(visible_tokens), encoder_project, preferred_element_type=jnp.float32
    ).astype(jnp.bfloat16)
    enc_pairs = lax.all_gather(enc_act[:, enc_width:], "seq", axis=0, tiled=True)
    enc_mix = attend(enc_act[:, :enc_width], enc_pairs[:, :enc_width], enc_pairs[:, enc_width:], EH)
    latent = (
        visible_tokens.astype(jnp.float32)
        + jnp.dot(enc_mix, encoder_output, preferred_element_type=jnp.float32)
    ).astype(jnp.bfloat16)
    peers = lax.axis_size("seq")
    vis_rows = latent.shape[0]
    visible_count = vis_rows * peers
    seen = restore_order < visible_count
    chosen = jnp.minimum(restore_order, visible_count - 1)
    local_embedded = jnp.dot(
        normalize(latent), decoder_embed, preferred_element_type=jnp.float32
    ).astype(jnp.bfloat16)
    capacity = max(1, vis_rows // peers)
    owners = chosen // vis_rows
    offsets = chosen % vis_rows
    owner_hot = (
        (owners[:, None] == jnp.arange(peers, dtype=jnp.int32)[None, :]) & seen[:, None]
    ).astype(jnp.int32)
    earlier = jnp.cumsum(owner_hot, axis=0) - owner_hot
    slot_index = jnp.sum(earlier * owner_hot, axis=1)
    flat_slot = owners * capacity + slot_index
    target_hot = (
        flat_slot[:, None] == jnp.arange(peers * capacity, dtype=jnp.int32)[None, :]
    ) & seen[:, None]
    requests = jnp.max(jnp.where(target_hot, offsets[:, None], -1), axis=0).reshape(peers, capacity)
    asked = lax.all_to_all(requests, "seq", split_axis=0, concat_axis=0, tiled=True)
    answers = jnp.take(local_embedded, jnp.maximum(asked, 0).reshape(-1), axis=0).reshape(
        peers, capacity, local_embedded.shape[1]
    )
    replies = lax.all_to_all(answers, "seq", split_axis=0, concat_axis=0, tiled=True)
    replies = replies.reshape(peers * capacity, local_embedded.shape[1])
    picked = jnp.take(replies, jnp.minimum(flat_slot, peers * capacity - 1), axis=0)
    filled = jnp.where(
        seen[:, None], picked.astype(jnp.float32), mask_token.astype(jnp.float32)[None, :]
    )
    dec_in = (filled + position_table.astype(jnp.float32)).astype(jnp.bfloat16)
    dec_act = jnp.dot(
        normalize(dec_in), decoder_project, preferred_element_type=jnp.float32
    ).astype(jnp.bfloat16)
    dec_pairs = lax.all_gather(dec_act[:, dec_width:], "seq", axis=0, tiled=True)
    dec_mix = attend(dec_act[:, :dec_width], dec_pairs[:, :dec_width], dec_pairs[:, dec_width:], DH)
    middle = (
        dec_in.astype(jnp.float32)
        + jnp.dot(dec_mix, decoder_output, preferred_element_type=jnp.float32)
    ).astype(jnp.bfloat16)
    hidden = jax.nn.gelu(
        jnp.dot(normalize(middle), expand_weight, preferred_element_type=jnp.float32),
        approximate=False,
    ).astype(jnp.bfloat16)
    decoded = (
        middle.astype(jnp.float32)
        + jnp.dot(hidden, shrink_weight, preferred_element_type=jnp.float32)
    ).astype(jnp.bfloat16)
    return (latent, decoded)


BF = jnp.bfloat16
F32 = jnp.float32
MESH = pl.DeviceIdType.MESH
LOG2E = 1.4426950408889634


def matmul(left, right):
    return jnp.dot(left, right, preferred_element_type=F32)


def matmul_nt(left, right):
    return lax.dot_general(left, right, (((1,), (1,)), ((), ())), preferred_element_type=F32)


def erf(value):
    value = jnp.clip(value, -3.832506856900711, 3.832506856900711)
    square = value * value
    top = jnp.full_like(value, 0.00022905065861350646)
    for coef in (0.0034082910107109506, 0.050955695062380861, 0.18520832239976145, 1.128379143519084):
        top = top * square + coef
    low = jnp.full_like(value, -1.1791602954361697e-7)
    for coef in (
        0.000023547966471313185,
        0.0010179625278914885,
        0.014070470171167667,
        0.11098505178285362,
        0.49746925110067538,
        1.0,
    ):
        low = low * square + coef
    return value * top / low


def lane_heads(rows, width, heads):
    lane = lax.broadcasted_iota(jnp.int32, (rows, width), 1)
    size = width // heads
    return [(lane >= h * size) & (lane < (h + 1) * size) for h in range(heads)]


def spread_heads(queries, heads):
    wide = queries.astype(F32)
    masks = lane_heads(*queries.shape, heads)
    return jnp.concatenate([jnp.where(mask, wide, 0.0).astype(BF) for mask in masks], axis=0)


def gather_heads(stacked, heads):
    rows, width = stacked.shape[0] // heads, stacked.shape[1]
    masks = lane_heads(rows, width, heads)
    total = jnp.zeros((rows, width), F32)
    for h, mask in enumerate(masks):
        total = jnp.where(mask, stacked[h * rows : (h + 1) * rows], total)
    return total.astype(BF)


class Gather:
    def __init__(self, buf, send, recv):
        self.buf, self.send, self.recv = buf, send, recv
        me = lax.axis_index("seq")
        self.group = lax.axis_index("groups")
        core = lax.rem(me, 2)
        x = lax.rem(lax.div(me, 2), 2)
        low = lax.rem(lax.div(me, 4), 2)
        high = lax.div(me, 8)

        def place(flip_high, flip_low, flip_x, flip_core):
            a = 1 - high if flip_high else high
            b = 1 - low if flip_low else low
            c = 1 - x if flip_x else x
            d = 1 - core if flip_core else core
            return a * 8 + b * 4 + c * 2 + d

        self.line = [place(k // 2, k % 2, 0, 0) for k in range(4)]
        self.line_x = [place(k // 2, k % 2, 1, 0) for k in range(4)]
        self.other = [place(k // 2, k % 2, q, 1) for q in range(2) for k in range(4)]
        self.me, self.x_peer, self.core_peer = me, self.line_x[0], self.other[0]
        self.peers = self.line[1:] + [self.x_peer, self.core_peer]
        self.started = []

    def copy(self, block, slot, peer):
        return pltpu.make_async_remote_copy(
            src_ref=self.buf.at[block],
            dst_ref=self.buf.at[block],
            send_sem=self.send.at[slot],
            recv_sem=self.recv.at[block],
            device_id=(self.group, peer),
            device_id_type=MESH,
        )

    def push(self, block, peer):
        copy = self.copy(block, len(self.started), peer)
        copy.start()
        self.started.append(copy)

    def arrive(self, block):
        self.copy(block, 0, self.core_peer).wait_recv()

    def start(self):
        for k in (3, 2, 1):
            self.push(self.me, self.line[k])
        self.push(self.me, self.x_peer)
        self.push(self.me, self.core_peer)

    def forward(self):
        for k in (1, 2, 3):
            self.arrive(self.line[k])
            self.push(self.line[k], self.x_peer)
            self.push(self.line[k], self.core_peer)

    def forward_x(self):
        for k in range(4):
            self.arrive(self.line_x[k])
            self.push(self.line_x[k], self.core_peer)

    def finish(self):
        for block in self.other:
            self.arrive(block)

    def sent(self):
        for copy in self.started:
            copy.wait_send()


def softmax_part(scores, factor):
    highest = jnp.max(scores, -1, keepdims=True)
    powers = jnp.exp2((scores - highest) * factor)
    return highest, powers.astype(BF), jnp.sum(powers, -1, keepdims=True)


def kernel(
    tokens, order, enc_proj, enc_out, embed, mask, pos, dec_proj, dec_out, expand, shrink,
    latent_out, decoded_out,
    w_enc, w_eo, w_emb, w_dec, w_do, w_ex, w_sh,
    kv, xb, eb, din, load_sem,
    kv_send, kv_recv, x_send, x_recv, e_send, e_recv,
):
    peers, vis, enc2 = kv.shape
    enc_width = enc2 // 2
    dec_width = w_do.shape[0]
    rows = pos.shape[0]
    hid = rows - vis
    visible_count = peers * vis

    g_kv = Gather(kv, kv_send, kv_recv)
    g_x = Gather(xb, x_send, x_recv)
    g_e = Gather(eb, e_send, e_recv)

    loads = [
        pltpu.make_async_copy(enc_proj.at[:, pl.ds(enc_width, enc2)], w_enc.at[:, pl.ds(enc_width, enc2)], load_sem.at[0]),
        pltpu.make_async_copy(dec_proj, w_dec, load_sem.at[1]),
        pltpu.make_async_copy(enc_proj.at[:, pl.ds(0, enc_width)], w_enc.at[:, pl.ds(0, enc_width)], load_sem.at[2]),
        pltpu.make_async_copy(enc_out, w_eo, load_sem.at[3]),
        pltpu.make_async_copy(embed, w_emb, load_sem.at[4]),
        pltpu.make_async_copy(dec_out, w_do, load_sem.at[5]),
        pltpu.make_async_copy(expand, w_ex, load_sem.at[6]),
        pltpu.make_async_copy(shrink, w_sh, load_sem.at[7]),
    ]
    loads[0].start()
    loads[1].start()

    barrier = pltpu.get_barrier_semaphore()
    for peer in g_kv.peers:
        pl.semaphore_signal(barrier, inc=1, device_id=(g_kv.group, peer), device_id_type=MESH)

    me = g_kv.me
    normed = normalize(tokens[...])
    loads[0].wait()
    kv[me] = matmul(normed, w_enc[:, enc_width:]).astype(BF)
    pl.semaphore_wait(barrier, len(g_kv.peers))
    g_kv.start()
    for load in loads[2:]:
        load.start()

    row_id = lax.broadcasted_iota(jnp.int32, (rows, rows), 0)
    col_id = lax.broadcasted_iota(jnp.int32, (rows, rows), 1)
    eye = row_id == col_id
    order_row = jnp.broadcast_to(order[...].astype(F32), (rows, rows))
    order_col = jnp.sum(jnp.where(eye, order_row, 0.0), axis=1, keepdims=True)
    seen_col = jnp.broadcast_to(order_col, (rows, rows)) < visible_count
    before = jnp.sum(jnp.where((row_id < col_id) & seen_col, 1.0, 0.0), axis=0, keepdims=True)
    before = jnp.broadcast_to(before, (rows, rows))
    slot = jnp.where(order_row < visible_count, before, vis + col_id.astype(F32) - before)
    to_slot = jnp.where(row_id.astype(F32) == slot, 1.0, 0.0)
    slot_col = jnp.sum(jnp.where(eye, slot, 0.0), axis=1, keepdims=True)
    from_slot = jnp.where(col_id.astype(F32) == slot_col, 1.0, 0.0).astype(BF)
    ranks = jnp.sum(to_slot * order_row, axis=1, keepdims=True)[:vis].astype(jnp.int32)
    ranks = jnp.broadcast_to(ranks, (vis, 128))
    upper = lax.div(ranks, 16)
    lower = (ranks - upper * 16).astype(F32).astype(BF)
    upper = upper.astype(F32).astype(BF)

    pos_slot = matmul(to_slot.astype(BF), pos[...])
    dec_hid = (pos_slot[vis:] + mask[...].astype(F32)).astype(BF)
    loads[1].wait()
    act_hid = matmul(normalize(dec_hid), w_dec[...]).astype(BF)
    xb[me, 0:vis, :] = pos_slot[:vis].astype(BF)
    xb[me, vis:rows, :] = act_hid[:, dec_width:]
    half = vis // 2
    xb[me, rows : rows + half, 0:128] = upper[:half]
    xb[me, rows : rows + half, 128:256] = upper[half:]
    xb[me, rows : rows + half, 256:384] = lower[:half]
    xb[me, rows : rows + half, 384:512] = lower[half:]
    g_x.start()

    loads[2].wait()
    enc_q = spread_heads(matmul(normed, w_enc[:, :enc_width]).astype(BF), EH)
    dec_qh = spread_heads(act_hid[:, :dec_width], DH)

    g_kv.forward()
    g_kv.forward_x()
    g_kv.finish()
    pairs = kv[...].reshape(visible_count, enc2)
    scores = matmul_nt(enc_q, pairs[:, :enc_width])
    _, powers, total = softmax_part(scores, (enc_width // EH) ** (-0.5) * LOG2E)
    mix = gather_heads(matmul(powers, pairs[:, enc_width:]) / total, EH)
    loads[3].wait()
    latent = (tokens[...].astype(F32) + matmul(mix, w_eo[...])).astype(BF)
    latent_out[...] = latent
    loads[4].wait()
    eb[me] = matmul(normalize(latent), w_emb[...]).astype(BF)
    g_e.start()

    g_x.forward()
    g_x.forward_x()
    g_x.finish()
    factor = (dec_width // DH) ** (-0.5) * LOG2E
    g_e.forward()
    g_e.forward_x()
    hid_keys = xb[:, vis:rows, 0:dec_width].reshape(peers * hid, dec_width)
    hid_values = xb[:, vis:rows, dec_width : 2 * dec_width].reshape(peers * hid, dec_width)
    top_hh, pow_hh, sum_hh = softmax_part(matmul_nt(dec_qh, hid_keys), factor)
    acc_hh = matmul(pow_hh, hid_values)

    g_e.finish()
    rank_hi = jnp.concatenate(
        [xb[:, rows : rows + half, 0:128].astype(F32), xb[:, rows : rows + half, 128:256].astype(F32)], axis=1
    ).reshape(visible_count, 128)
    rank_lo = jnp.concatenate(
        [xb[:, rows : rows + half, 256:384].astype(F32), xb[:, rows : rows + half, 384:512].astype(F32)], axis=1
    ).reshape(visible_count, 128)
    rank = rank_hi * 16.0 + rank_lo
    lane = lax.broadcasted_iota(jnp.int32, (visible_count, 128), 1).astype(F32)
    hot = jnp.concatenate(
        [jnp.where(rank == lane + 128.0 * k, 1.0, 0.0).astype(BF) for k in range(visible_count // 128)], axis=1
    )
    width = eb.shape[2]
    picked = matmul(hot, eb[...].reshape(visible_count, width))
    dec_vis = (picked + xb[:, 0:vis, :].reshape(visible_count, width).astype(F32)).astype(BF)
    din[...] = dec_vis.reshape(peers, vis, width)
    pairs_vis = matmul(normalize(dec_vis), w_dec[:, dec_width:]).astype(BF)
    own_vis = din[me]
    dec_qv = spread_heads(matmul(normalize(own_vis), w_dec[:, :dec_width]).astype(BF), DH)
    vis_keys, vis_values = pairs_vis[:, :dec_width], pairs_vis[:, dec_width:]

    def merge(scores, top, total, acc):
        highest = jnp.maximum(top, jnp.max(scores, -1, keepdims=True))
        powers = jnp.exp2((scores - highest) * factor)
        fade = jnp.exp2((top - highest) * factor)
        total = total * fade + jnp.sum(powers, -1, keepdims=True)
        return (acc * fade + matmul(powers.astype(BF), vis_values)) / total

    mix_h = gather_heads(merge(matmul_nt(dec_qh, vis_keys), top_hh, sum_hh, acc_hh), DH)
    top_vh, pow_vh, sum_vh = softmax_part(matmul_nt(dec_qv, hid_keys), factor)
    acc_vh = matmul(pow_vh, hid_values)
    mix_v = gather_heads(merge(matmul_nt(dec_qv, vis_keys), top_vh, sum_vh, acc_vh), DH)

    dec_in = jnp.concatenate([own_vis, dec_hid], axis=0)
    dec_mix = jnp.concatenate([mix_v, mix_h], axis=0)
    loads[5].wait()
    middle = (dec_in.astype(F32) + matmul(dec_mix, w_do[...])).astype(BF)
    loads[6].wait()
    wide = matmul(normalize(middle), w_ex[...])
    hidden = (0.5 * wide * (1.0 + erf(wide * 0.7071067811865476))).astype(BF)
    loads[7].wait()
    decoded = (middle.astype(F32) + matmul(hidden, w_sh[...])).astype(BF)
    decoded_out[...] = matmul(from_slot, decoded).astype(BF)
    g_kv.sent()
    g_x.sent()
    g_e.sent()


def on_device(peers, tokens, order, enc_proj, enc_out, embed, mask, pos, dec_proj, dec_out, expand, shrink):
    vis, rows, width = tokens.shape[0], pos.shape[0], pos.shape[1]
    weights = (enc_proj, enc_out, embed, dec_proj, dec_out, expand, shrink)
    vmem = pl.BlockSpec(memory_space=pltpu.VMEM)
    anywhere = pl.BlockSpec(memory_space=pl.ANY)
    return pl.pallas_call(
        kernel,
        out_shape=(
            jax.ShapeDtypeStruct(tokens.shape, BF),
            jax.ShapeDtypeStruct(pos.shape, BF),
        ),
        in_specs=[vmem, vmem, anywhere, anywhere, anywhere, vmem, vmem, anywhere, anywhere, anywhere, anywhere],
        out_specs=(vmem, vmem),
        scratch_shapes=[pltpu.VMEM(w.shape, BF) for w in weights]
        + [
            pltpu.VMEM((peers, vis, 2 * enc_out.shape[0]), BF),
            pltpu.VMEM((peers, rows + vis // 2, width), BF),
            pltpu.VMEM((peers, vis, width), BF),
            pltpu.VMEM((peers, vis, width), BF),
            pltpu.SemaphoreType.DMA((8,)),
        ]
        + [pltpu.SemaphoreType.DMA((n,)) for _ in range(3) for n in (15, peers)],
        compiler_params=pltpu.CompilerParams(
            collective_id=0, has_side_effects=True, vmem_limit_bytes=56 * 1024 * 1024
        ),
    )(tokens, order.reshape(1, rows), enc_proj, enc_out, embed, mask.reshape(1, width), pos,
      dec_proj, dec_out, expand, shrink)


def solution(mesh):
    in_specs = (
        P(("groups", "seq"), None),
        P(("groups", "seq")),
        P(),
        P(),
        P(),
        P(),
        P("seq", None),
        P(),
        P(),
        P(),
        P(),
    )
    out_specs = (P(("groups", "seq"), None), P(("groups", "seq"), None))
    peers = mesh.shape["seq"]
    body = functools.partial(on_device, peers) if peers == 16 else on_device_plain
    return jax.shard_map(
        body, mesh=mesh, in_specs=in_specs, out_specs=out_specs, check_vma=False
    )
```

```python
import functools

import jax
import jax.numpy as jnp
from jax import lax
from jax.experimental import pallas as pl
from jax.experimental.pallas import tpu as pltpu
from jax.sharding import PartitionSpec as P

EH = 8
DH = 8


def normalize(values):
    values = values.astype(jnp.float32)
    centre = values - jnp.mean(values, -1, keepdims=True)
    spread = jnp.mean(centre * centre, -1, keepdims=True)
    return (centre * lax.rsqrt(spread + 1e-06)).astype(jnp.bfloat16)


def attend(queries, keys, values, heads):
    total, width = queries.shape
    size = width // heads
    query_heads = queries.reshape(total, heads, size).transpose(1, 0, 2)
    key_heads = keys.reshape(keys.shape[0], heads, size).transpose(1, 0, 2)
    value_heads = values.reshape(values.shape[0], heads, size).transpose(1, 0, 2)

    def one_head(operands):
        query_part, key_part, value_part = operands
        scores = lax.dot_general(
            query_part, key_part, (((1,), (1,)), ((), ())), preferred_element_type=jnp.float32
        ) * size ** (-0.5)
        highest = jnp.max(scores, -1, keepdims=True)
        powers = jnp.exp(scores - highest)
        weights = (powers / jnp.sum(powers, -1, keepdims=True)).astype(jnp.bfloat16)
        return jnp.dot(weights, value_part, preferred_element_type=jnp.float32).astype(jnp.bfloat16)

    result = lax.map(one_head, (query_heads, key_heads, value_heads))
    return result.transpose(1, 0, 2).reshape(total, width)


def on_device_plain(
    visible_tokens,
    restore_order,
    encoder_project,
    encoder_output,
    decoder_embed,
    mask_token,
    position_table,
    decoder_project,
    decoder_output,
    expand_weight,
    shrink_weight,
):
    enc_width = encoder_output.shape[0]
    dec_width = decoder_output.shape[0]
    enc_act = jnp.dot(
        normalize(visible_tokens), encoder_project, preferred_element_type=jnp.float32
    ).astype(jnp.bfloat16)
    enc_pairs = lax.all_gather(enc_act[:, enc_width:], "seq", axis=0, tiled=True)
    enc_mix = attend(enc_act[:, :enc_width], enc_pairs[:, :enc_width], enc_pairs[:, enc_width:], EH)
    latent = (
        visible_tokens.astype(jnp.float32)
        + jnp.dot(enc_mix, encoder_output, preferred_element_type=jnp.float32)
    ).astype(jnp.bfloat16)
    peers = lax.axis_size("seq")
    vis_rows = latent.shape[0]
    visible_count = vis_rows * peers
    seen = restore_order < visible_count
    chosen = jnp.minimum(restore_order, visible_count - 1)
    local_embedded = jnp.dot(
        normalize(latent), decoder_embed, preferred_element_type=jnp.float32
    ).astype(jnp.bfloat16)
    capacity = max(1, vis_rows // peers)
    owners = chosen // vis_rows
    offsets = chosen % vis_rows
    owner_hot = (
        (owners[:, None] == jnp.arange(peers, dtype=jnp.int32)[None, :]) & seen[:, None]
    ).astype(jnp.int32)
    earlier = jnp.cumsum(owner_hot, axis=0) - owner_hot
    slot_index = jnp.sum(earlier * owner_hot, axis=1)
    flat_slot = owners * capacity + slot_index
    target_hot = (
        flat_slot[:, None] == jnp.arange(peers * capacity, dtype=jnp.int32)[None, :]
    ) & seen[:, None]
    requests = jnp.max(jnp.where(target_hot, offsets[:, None], -1), axis=0).reshape(peers, capacity)
    asked = lax.all_to_all(requests, "seq", split_axis=0, concat_axis=0, tiled=True)
    answers = jnp.take(local_embedded, jnp.maximum(asked, 0).reshape(-1), axis=0).reshape(
        peers, capacity, local_embedded.shape[1]
    )
    replies = lax.all_to_all(answers, "seq", split_axis=0, concat_axis=0, tiled=True)
    replies = replies.reshape(peers * capacity, local_embedded.shape[1])
    picked = jnp.take(replies, jnp.minimum(flat_slot, peers * capacity - 1), axis=0)
    filled = jnp.where(
        seen[:, None], picked.astype(jnp.float32), mask_token.astype(jnp.float32)[None, :]
    )
    dec_in = (filled + position_table.astype(jnp.float32)).astype(jnp.bfloat16)
    dec_act = jnp.dot(
        normalize(dec_in), decoder_project, preferred_element_type=jnp.float32
    ).astype(jnp.bfloat16)
    dec_pairs = lax.all_gather(dec_act[:, dec_width:], "seq", axis=0, tiled=True)
    dec_mix = attend(dec_act[:, :dec_width], dec_pairs[:, :dec_width], dec_pairs[:, dec_width:], DH)
    middle = (
        dec_in.astype(jnp.float32)
        + jnp.dot(dec_mix, decoder_output, preferred_element_type=jnp.float32)
    ).astype(jnp.bfloat16)
    hidden = jax.nn.gelu(
        jnp.dot(normalize(middle), expand_weight, preferred_element_type=jnp.float32),
        approximate=False,
    ).astype(jnp.bfloat16)
    decoded = (
        middle.astype(jnp.float32)
        + jnp.dot(hidden, shrink_weight, preferred_element_type=jnp.float32)
    ).astype(jnp.bfloat16)
    return (latent, decoded)


BF = jnp.bfloat16
F32 = jnp.float32
MESH = pl.DeviceIdType.MESH
LOG2E = 1.4426950408889634


def matmul(left, right):
    return jnp.dot(left, right, preferred_element_type=F32)


def matmul_nt(left, right):
    return lax.dot_general(left, right, (((1,), (1,)), ((), ())), preferred_element_type=F32)


def erf(value):
    value = jnp.clip(value, -3.832506856900711, 3.832506856900711)
    square = value * value
    top = jnp.full_like(value, 0.00022905065861350646)
    for coef in (0.0034082910107109506, 0.050955695062380861, 0.18520832239976145, 1.128379143519084):
        top = top * square + coef
    low = jnp.full_like(value, -1.1791602954361697e-7)
    for coef in (
        0.000023547966471313185,
        0.0010179625278914885,
        0.014070470171167667,
        0.11098505178285362,
        0.49746925110067538,
        1.0,
    ):
        low = low * square + coef
    return value * top / low


def lane_heads(rows, width, heads):
    lane = lax.broadcasted_iota(jnp.int32, (rows, width), 1)
    size = width // heads
    return [(lane >= h * size) & (lane < (h + 1) * size) for h in range(heads)]


def spread_heads(queries, heads):
    wide = queries.astype(F32)
    masks = lane_heads(*queries.shape, heads)
    return jnp.concatenate([jnp.where(mask, wide, 0.0).astype(BF) for mask in masks], axis=0)


def gather_heads(stacked, heads):
    rows, width = stacked.shape[0] // heads, stacked.shape[1]
    masks = lane_heads(rows, width, heads)
    total = jnp.zeros((rows, width), F32)
    for h, mask in enumerate(masks):
        total = jnp.where(mask, stacked[h * rows : (h + 1) * rows], total)
    return total.astype(BF)


class Gather:
    def __init__(self, buf, send, recv):
        self.buf, self.send, self.recv = buf, send, recv
        me = lax.axis_index("seq")
        self.group = lax.axis_index("groups")
        core = lax.rem(me, 2)
        x = lax.rem(lax.div(me, 2), 2)
        low = lax.rem(lax.div(me, 4), 2)
        high = lax.div(me, 8)

        def place(flip_high, flip_low, flip_x, flip_core):
            a = 1 - high if flip_high else high
            b = 1 - low if flip_low else low
            c = 1 - x if flip_x else x
            d = 1 - core if flip_core else core
            return a * 8 + b * 4 + c * 2 + d

        self.line = [place(k // 2, k % 2, 0, 0) for k in range(4)]
        self.line_x = [place(k // 2, k % 2, 1, 0) for k in range(4)]
        self.other = [place(k // 2, k % 2, q, 1) for q in range(2) for k in range(4)]
        self.me, self.x_peer, self.core_peer = me, self.line_x[0], self.other[0]
        self.peers = self.line[1:] + [self.x_peer, self.core_peer]
        self.started = []

    def copy(self, block, slot, peer):
        return pltpu.make_async_remote_copy(
            src_ref=self.buf.at[block],
            dst_ref=self.buf.at[block],
            send_sem=self.send.at[slot],
            recv_sem=self.recv.at[block],
            device_id=(self.group, peer),
            device_id_type=MESH,
        )

    def push(self, block, peer):
        copy = self.copy(block, len(self.started), peer)
        copy.start()
        self.started.append(copy)

    def arrive(self, block):
        self.copy(block, 0, self.core_peer).wait_recv()

    def start(self):
        for k in (3, 2, 1):
            self.push(self.me, self.line[k])
        self.push(self.me, self.x_peer)
        self.push(self.me, self.core_peer)

    def forward(self, steps=(1, 2, 3)):
        for k in steps:
            self.arrive(self.line[k])
            self.push(self.line[k], self.x_peer)
            self.push(self.line[k], self.core_peer)

    def forward_x(self):
        for k in range(4):
            self.arrive(self.line_x[k])
            self.push(self.line_x[k], self.core_peer)

    def finish(self):
        for block in self.other:
            self.arrive(block)

    def sent(self):
        for copy in self.started:
            copy.wait_send()


def softmax_part(scores, factor):
    highest = jnp.max(scores, -1, keepdims=True)
    powers = jnp.exp2((scores - highest) * factor)
    return highest, powers.astype(BF), jnp.sum(powers, -1, keepdims=True)


def kernel(
    tokens, order, enc_proj, enc_out, embed, mask, pos, dec_proj, dec_out, expand, shrink,
    latent_out, decoded_out,
    w_enc, w_eo, w_emb, w_dec, w_do, w_ex, w_sh,
    tb, xb, eb, din, load_sem,
    t_send, t_recv, x_send, x_recv, e_send, e_recv,
):
    peers, vis, _ = tb.shape
    enc_width = w_eo.shape[0]
    enc2 = 2 * enc_width
    dec_width = w_do.shape[0]
    rows = pos.shape[0]
    hid = rows - vis
    visible_count = peers * vis

    g_t = Gather(tb, t_send, t_recv)
    g_x = Gather(xb, x_send, x_recv)
    g_e = Gather(eb, e_send, e_recv)

    loads = [
        pltpu.make_async_copy(dec_proj, w_dec, load_sem.at[0]),
        pltpu.make_async_copy(enc_proj, w_enc, load_sem.at[1]),
        pltpu.make_async_copy(enc_out, w_eo, load_sem.at[2]),
        pltpu.make_async_copy(embed, w_emb, load_sem.at[3]),
        pltpu.make_async_copy(dec_out, w_do, load_sem.at[4]),
        pltpu.make_async_copy(expand, w_ex, load_sem.at[5]),
        pltpu.make_async_copy(shrink, w_sh, load_sem.at[6]),
    ]
    barrier = pltpu.get_barrier_semaphore()
    for peer in g_t.peers:
        pl.semaphore_signal(barrier, inc=1, device_id=(g_t.group, peer), device_id_type=MESH)
    for load in loads:
        load.start()

    me = g_t.me
    tb[me] = tokens[...]
    pl.semaphore_wait(barrier, len(g_t.peers))
    g_t.start()

    row_id = lax.broadcasted_iota(jnp.int32, (rows, rows), 0)
    col_id = lax.broadcasted_iota(jnp.int32, (rows, rows), 1)
    eye = row_id == col_id
    order_row = jnp.broadcast_to(order[...].astype(F32), (rows, rows))
    order_col = jnp.sum(jnp.where(eye, order_row, 0.0), axis=1, keepdims=True)
    seen_col = jnp.broadcast_to(order_col, (rows, rows)) < visible_count
    before = jnp.sum(jnp.where((row_id < col_id) & seen_col, 1.0, 0.0), axis=0, keepdims=True)
    before = jnp.broadcast_to(before, (rows, rows))
    slot = jnp.where(order_row < visible_count, before, vis + col_id.astype(F32) - before)
    to_slot = jnp.where(row_id.astype(F32) == slot, 1.0, 0.0)
    slot_col = jnp.sum(jnp.where(eye, slot, 0.0), axis=1, keepdims=True)
    from_slot = jnp.where(col_id.astype(F32) == slot_col, 1.0, 0.0).astype(BF)
    ranks = jnp.sum(to_slot * order_row, axis=1, keepdims=True)[:vis].astype(jnp.int32)
    ranks = jnp.broadcast_to(ranks, (vis, 128))
    upper = lax.div(ranks, 16)
    lower = (ranks - upper * 16).astype(F32).astype(BF)
    upper = upper.astype(F32).astype(BF)

    pos_slot = matmul(to_slot.astype(BF), pos[...])
    dec_hid = (pos_slot[vis:] + mask[...].astype(F32).reshape(1, -1)).astype(BF)
    loads[0].wait()
    act_hid = matmul(normalize(dec_hid), w_dec[...]).astype(BF)
    xb[me, 0:vis, :] = pos_slot[:vis].astype(BF)
    xb[me, vis:rows, :] = act_hid[:, dec_width:]
    half = vis // 2
    xb[me, rows : rows + half, 0:128] = upper[:half]
    xb[me, rows : rows + half, 128:256] = upper[half:]
    xb[me, rows : rows + half, 256:384] = lower[:half]
    xb[me, rows : rows + half, 384:512] = lower[half:]
    g_x.push(me, g_x.x_peer)
    g_x.push(me, g_x.line[1])

    def pairs_of(blocks):
        rows_in = jnp.concatenate([tb[block] for block in blocks], axis=0)
        return matmul(normalize(rows_in), w_enc[:, enc_width:]).astype(BF)

    loads[1].wait()
    enc_q = spread_heads(matmul(normalize(tokens[...]), w_enc[:, :enc_width]).astype(BF), EH)
    dec_qh = spread_heads(act_hid[:, :dec_width], DH)

    g_t.forward()
    g_x.push(me, g_x.line[2])
    g_x.push(me, g_x.core_peer)
    pairs = [pairs_of(g_t.line)]
    g_t.forward_x()
    g_x.push(me, g_x.line[3])
    pairs.append(pairs_of(g_t.line_x))
    g_x.forward((1,))
    g_t.finish()
    pairs.append(pairs_of(g_t.other))
    g_x.forward((2,))
    pairs = jnp.concatenate(pairs, axis=0)
    scores = matmul_nt(enc_q, pairs[:, :enc_width])
    _, powers, total = softmax_part(scores, (enc_width // EH) ** (-0.5) * LOG2E)
    mix = gather_heads(matmul(powers, pairs[:, enc_width:]) / total, EH)
    loads[2].wait()
    latent = (tokens[...].astype(F32) + matmul(mix, w_eo[...])).astype(BF)
    latent_out[...] = latent
    loads[3].wait()
    eb[me] = matmul(normalize(latent), w_emb[...]).astype(BF)
    g_e.start()

    g_x.forward((3,))
    g_e.forward()
    g_e.forward_x()
    g_x.forward_x()
    g_x.finish()
    factor = (dec_width // DH) ** (-0.5) * LOG2E
    hid_keys = xb[:, vis:rows, 0:dec_width].reshape(peers * hid, dec_width)
    hid_values = xb[:, vis:rows, dec_width : 2 * dec_width].reshape(peers * hid, dec_width)
    top_hh, pow_hh, sum_hh = softmax_part(matmul_nt(dec_qh, hid_keys), factor)
    acc_hh = matmul(pow_hh, hid_values)

    g_e.finish()
    rank_hi = jnp.concatenate(
        [xb[:, rows : rows + half, 0:128].astype(F32), xb[:, rows : rows + half, 128:256].astype(F32)], axis=1
    ).reshape(visible_count, 128)
    rank_lo = jnp.concatenate(
        [xb[:, rows : rows + half, 256:384].astype(F32), xb[:, rows : rows + half, 384:512].astype(F32)], axis=1
    ).reshape(visible_count, 128)
    rank = rank_hi * 16.0 + rank_lo
    lane = lax.broadcasted_iota(jnp.int32, (visible_count, 128), 1).astype(F32)
    hot = jnp.concatenate(
        [jnp.where(rank == lane + 128.0 * k, 1.0, 0.0).astype(BF) for k in range(visible_count // 128)], axis=1
    )
    width = eb.shape[2]
    picked = matmul(hot, eb[...].reshape(visible_count, width))
    dec_vis = (picked + xb[:, 0:vis, :].reshape(visible_count, width).astype(F32)).astype(BF)
    din[...] = dec_vis.reshape(peers, vis, width)
    pairs_vis = matmul(normalize(dec_vis), w_dec[:, dec_width:]).astype(BF)
    own_vis = din[me]
    dec_qv = spread_heads(matmul(normalize(own_vis), w_dec[:, :dec_width]).astype(BF), DH)
    vis_keys, vis_values = pairs_vis[:, :dec_width], pairs_vis[:, dec_width:]

    def merge(scores, top, total, acc):
        highest = jnp.maximum(top, jnp.max(scores, -1, keepdims=True))
        powers = jnp.exp2((scores - highest) * factor)
        fade = jnp.exp2((top - highest) * factor)
        total = total * fade + jnp.sum(powers, -1, keepdims=True)
        return (acc * fade + matmul(powers.astype(BF), vis_values)) / total

    mix_h = gather_heads(merge(matmul_nt(dec_qh, vis_keys), top_hh, sum_hh, acc_hh), DH)
    top_vh, pow_vh, sum_vh = softmax_part(matmul_nt(dec_qv, hid_keys), factor)
    acc_vh = matmul(pow_vh, hid_values)
    mix_v = gather_heads(merge(matmul_nt(dec_qv, vis_keys), top_vh, sum_vh, acc_vh), DH)

    dec_in = jnp.concatenate([own_vis, dec_hid], axis=0)
    dec_mix = jnp.concatenate([mix_v, mix_h], axis=0)
    loads[4].wait()
    middle = (dec_in.astype(F32) + matmul(dec_mix, w_do[...])).astype(BF)
    loads[5].wait()
    wide = matmul(normalize(middle), w_ex[...])
    hidden = (0.5 * wide * (1.0 + erf(wide * 0.7071067811865476))).astype(BF)
    loads[6].wait()
    decoded = (middle.astype(F32) + matmul(hidden, w_sh[...])).astype(BF)
    decoded_out[...] = matmul(from_slot, decoded).astype(BF)
    g_t.sent()
    g_x.sent()
    g_e.sent()


def on_device(peers, tokens, order, enc_proj, enc_out, embed, mask, pos, dec_proj, dec_out, expand, shrink):
    vis, rows, width = tokens.shape[0], pos.shape[0], pos.shape[1]
    weights = (enc_proj, enc_out, embed, dec_proj, dec_out, expand, shrink)
    vmem = pl.BlockSpec(memory_space=pltpu.VMEM)
    anywhere = pl.BlockSpec(memory_space=pl.ANY)
    return pl.pallas_call(
        kernel,
        out_shape=(
            jax.ShapeDtypeStruct(tokens.shape, BF),
            jax.ShapeDtypeStruct(pos.shape, BF),
        ),
        in_specs=[vmem, vmem, anywhere, anywhere, anywhere, vmem, vmem, anywhere, anywhere, anywhere, anywhere],
        out_specs=(vmem, vmem),
        scratch_shapes=[pltpu.VMEM(w.shape, BF) for w in weights]
        + [
            pltpu.VMEM((peers, vis, tokens.shape[1]), BF),
            pltpu.VMEM((peers, rows + vis // 2, width), BF),
            pltpu.VMEM((peers, vis, width), BF),
            pltpu.VMEM((peers, vis, width), BF),
            pltpu.SemaphoreType.DMA((7,)),
        ]
        + [pltpu.SemaphoreType.DMA((n,)) for _ in range(3) for n in (15, peers)],
        compiler_params=pltpu.CompilerParams(
            collective_id=0, has_side_effects=True, vmem_limit_bytes=56 * 1024 * 1024
        ),
    )(tokens, order.reshape(1, rows), enc_proj, enc_out, embed, mask, pos,
      dec_proj, dec_out, expand, shrink)


def solution(mesh):
    in_specs = (
        P(("groups", "seq"), None),
        P(("groups", "seq")),
        P(),
        P(),
        P(),
        P(),
        P("seq", None),
        P(),
        P(),
        P(),
        P(),
    )
    out_specs = (P(("groups", "seq"), None), P(("groups", "seq"), None))
    peers = mesh.shape["seq"]
    body = functools.partial(on_device, peers) if peers == 16 else on_device_plain
    return jax.shard_map(
        body, mesh=mesh, in_specs=in_specs, out_specs=out_specs, check_vma=False
    )
```

```python
import functools

import jax
import jax.numpy as jnp
from jax import lax
from jax.experimental import pallas as pl
from jax.experimental.pallas import tpu as pltpu
from jax.sharding import PartitionSpec as P

EH = 8
DH = 8


def normalize(values):
    values = values.astype(jnp.float32)
    centre = values - jnp.mean(values, -1, keepdims=True)
    spread = jnp.mean(centre * centre, -1, keepdims=True)
    return (centre * lax.rsqrt(spread + 1e-06)).astype(jnp.bfloat16)


def attend(queries, keys, values, heads):
    total, width = queries.shape
    size = width // heads
    query_heads = queries.reshape(total, heads, size).transpose(1, 0, 2)
    key_heads = keys.reshape(keys.shape[0], heads, size).transpose(1, 0, 2)
    value_heads = values.reshape(values.shape[0], heads, size).transpose(1, 0, 2)

    def one_head(operands):
        query_part, key_part, value_part = operands
        scores = lax.dot_general(
            query_part, key_part, (((1,), (1,)), ((), ())), preferred_element_type=jnp.float32
        ) * size ** (-0.5)
        highest = jnp.max(scores, -1, keepdims=True)
        powers = jnp.exp(scores - highest)
        weights = (powers / jnp.sum(powers, -1, keepdims=True)).astype(jnp.bfloat16)
        return jnp.dot(weights, value_part, preferred_element_type=jnp.float32).astype(jnp.bfloat16)

    result = lax.map(one_head, (query_heads, key_heads, value_heads))
    return result.transpose(1, 0, 2).reshape(total, width)


def on_device_plain(
    visible_tokens,
    restore_order,
    encoder_project,
    encoder_output,
    decoder_embed,
    mask_token,
    position_table,
    decoder_project,
    decoder_output,
    expand_weight,
    shrink_weight,
):
    enc_width = encoder_output.shape[0]
    dec_width = decoder_output.shape[0]
    enc_act = jnp.dot(
        normalize(visible_tokens), encoder_project, preferred_element_type=jnp.float32
    ).astype(jnp.bfloat16)
    enc_pairs = lax.all_gather(enc_act[:, enc_width:], "seq", axis=0, tiled=True)
    enc_mix = attend(enc_act[:, :enc_width], enc_pairs[:, :enc_width], enc_pairs[:, enc_width:], EH)
    latent = (
        visible_tokens.astype(jnp.float32)
        + jnp.dot(enc_mix, encoder_output, preferred_element_type=jnp.float32)
    ).astype(jnp.bfloat16)
    peers = lax.axis_size("seq")
    vis_rows = latent.shape[0]
    visible_count = vis_rows * peers
    seen = restore_order < visible_count
    chosen = jnp.minimum(restore_order, visible_count - 1)
    local_embedded = jnp.dot(
        normalize(latent), decoder_embed, preferred_element_type=jnp.float32
    ).astype(jnp.bfloat16)
    capacity = max(1, vis_rows // peers)
    owners = chosen // vis_rows
    offsets = chosen % vis_rows
    owner_hot = (
        (owners[:, None] == jnp.arange(peers, dtype=jnp.int32)[None, :]) & seen[:, None]
    ).astype(jnp.int32)
    earlier = jnp.cumsum(owner_hot, axis=0) - owner_hot
    slot_index = jnp.sum(earlier * owner_hot, axis=1)
    flat_slot = owners * capacity + slot_index
    target_hot = (
        flat_slot[:, None] == jnp.arange(peers * capacity, dtype=jnp.int32)[None, :]
    ) & seen[:, None]
    requests = jnp.max(jnp.where(target_hot, offsets[:, None], -1), axis=0).reshape(peers, capacity)
    asked = lax.all_to_all(requests, "seq", split_axis=0, concat_axis=0, tiled=True)
    answers = jnp.take(local_embedded, jnp.maximum(asked, 0).reshape(-1), axis=0).reshape(
        peers, capacity, local_embedded.shape[1]
    )
    replies = lax.all_to_all(answers, "seq", split_axis=0, concat_axis=0, tiled=True)
    replies = replies.reshape(peers * capacity, local_embedded.shape[1])
    picked = jnp.take(replies, jnp.minimum(flat_slot, peers * capacity - 1), axis=0)
    filled = jnp.where(
        seen[:, None], picked.astype(jnp.float32), mask_token.astype(jnp.float32)[None, :]
    )
    dec_in = (filled + position_table.astype(jnp.float32)).astype(jnp.bfloat16)
    dec_act = jnp.dot(
        normalize(dec_in), decoder_project, preferred_element_type=jnp.float32
    ).astype(jnp.bfloat16)
    dec_pairs = lax.all_gather(dec_act[:, dec_width:], "seq", axis=0, tiled=True)
    dec_mix = attend(dec_act[:, :dec_width], dec_pairs[:, :dec_width], dec_pairs[:, dec_width:], DH)
    middle = (
        dec_in.astype(jnp.float32)
        + jnp.dot(dec_mix, decoder_output, preferred_element_type=jnp.float32)
    ).astype(jnp.bfloat16)
    hidden = jax.nn.gelu(
        jnp.dot(normalize(middle), expand_weight, preferred_element_type=jnp.float32),
        approximate=False,
    ).astype(jnp.bfloat16)
    decoded = (
        middle.astype(jnp.float32)
        + jnp.dot(hidden, shrink_weight, preferred_element_type=jnp.float32)
    ).astype(jnp.bfloat16)
    return (latent, decoded)


BF = jnp.bfloat16
F32 = jnp.float32
MESH = pl.DeviceIdType.MESH
LOG2E = 1.4426950408889634


def matmul(left, right):
    return jnp.dot(left, right, preferred_element_type=F32)


def matmul_nt(left, right):
    return lax.dot_general(left, right, (((1,), (1,)), ((), ())), preferred_element_type=F32)


def erf(value):
    value = jnp.clip(value, -3.832506856900711, 3.832506856900711)
    square = value * value
    top = jnp.full_like(value, 0.00022905065861350646)
    for coef in (0.0034082910107109506, 0.050955695062380861, 0.18520832239976145, 1.128379143519084):
        top = top * square + coef
    low = jnp.full_like(value, -1.1791602954361697e-7)
    for coef in (
        0.000023547966471313185,
        0.0010179625278914885,
        0.014070470171167667,
        0.11098505178285362,
        0.49746925110067538,
        1.0,
    ):
        low = low * square + coef
    return value * top / low


def lane_heads(rows, width, heads):
    lane = lax.broadcasted_iota(jnp.int32, (rows, width), 1)
    size = width // heads
    return [(lane >= h * size) & (lane < (h + 1) * size) for h in range(heads)]


def spread_heads(queries, heads):
    wide = queries.astype(F32)
    masks = lane_heads(*queries.shape, heads)
    return jnp.concatenate([jnp.where(mask, wide, 0.0).astype(BF) for mask in masks], axis=0)


def gather_heads(stacked, heads):
    rows, width = stacked.shape[0] // heads, stacked.shape[1]
    masks = lane_heads(rows, width, heads)
    total = jnp.zeros((rows, width), F32)
    for h, mask in enumerate(masks):
        total = jnp.where(mask, stacked[h * rows : (h + 1) * rows], total)
    return total.astype(BF)


class Gather:
    def __init__(self, buf, send, recv):
        self.buf, self.send, self.recv = buf, send, recv
        me = lax.axis_index("seq")
        self.group = lax.axis_index("groups")
        core = lax.rem(me, 2)
        x = lax.rem(lax.div(me, 2), 2)
        low = lax.rem(lax.div(me, 4), 2)
        high = lax.div(me, 8)

        def place(flip_high, flip_low, flip_x, flip_core):
            a = 1 - high if flip_high else high
            b = 1 - low if flip_low else low
            c = 1 - x if flip_x else x
            d = 1 - core if flip_core else core
            return a * 8 + b * 4 + c * 2 + d

        self.line = [place(k // 2, k % 2, 0, 0) for k in range(4)]
        self.line_x = [place(k // 2, k % 2, 1, 0) for k in range(4)]
        self.other = [place(k // 2, k % 2, q, 1) for q in range(2) for k in range(4)]
        self.me, self.x_peer, self.core_peer = me, self.line_x[0], self.other[0]
        self.peers = self.line[1:] + [self.x_peer, self.core_peer]
        self.started = []

    def copy(self, block, slot, peer):
        return pltpu.make_async_remote_copy(
            src_ref=self.buf.at[block],
            dst_ref=self.buf.at[block],
            send_sem=self.send.at[slot],
            recv_sem=self.recv.at[block],
            device_id=(self.group, peer),
            device_id_type=MESH,
        )

    def push(self, block, peer):
        copy = self.copy(block, len(self.started), peer)
        copy.start()
        self.started.append(copy)

    def arrive(self, block):
        self.copy(block, 0, self.core_peer).wait_recv()

    def start(self):
        self.push(self.me, self.x_peer)
        for k in (1, 2, 3):
            self.push(self.me, self.line[k])
        self.push(self.me, self.core_peer)

    def forward(self, steps=(1, 2, 3)):
        for k in steps:
            self.arrive(self.line[k])
            self.push(self.line[k], self.x_peer)
            self.push(self.line[k], self.core_peer)

    def forward_x(self):
        for k in range(4):
            self.arrive(self.line_x[k])
            self.push(self.line_x[k], self.core_peer)

    def finish(self):
        for block in self.other:
            self.arrive(block)

    def sent(self):
        for copy in self.started:
            copy.wait_send()


def softmax_part(scores, factor):
    highest = jnp.max(scores, -1, keepdims=True)
    powers = jnp.exp2((scores - highest) * factor)
    return highest, powers.astype(BF), jnp.sum(powers, -1, keepdims=True)


def kernel(
    tokens, order, enc_proj, enc_out, embed, mask, pos, dec_proj, dec_out, expand, shrink,
    latent_out, decoded_out,
    w_enc, w_eo, w_emb, w_dec, w_do, w_ex, w_sh,
    tb, xb, eb, din, load_sem,
    t_send, t_recv, x_send, x_recv, e_send, e_recv,
):
    peers, vis, _ = tb.shape
    enc_width = w_eo.shape[0]
    enc2 = 2 * enc_width
    dec_width = w_do.shape[0]
    rows = pos.shape[0]
    hid = rows - vis
    visible_count = peers * vis

    g_t = Gather(tb, t_send, t_recv)
    g_x = Gather(xb, x_send, x_recv)
    g_e = Gather(eb, e_send, e_recv)

    loads = [
        pltpu.make_async_copy(dec_proj, w_dec, load_sem.at[0]),
        pltpu.make_async_copy(enc_proj, w_enc, load_sem.at[1]),
        pltpu.make_async_copy(enc_out, w_eo, load_sem.at[2]),
        pltpu.make_async_copy(embed, w_emb, load_sem.at[3]),
        pltpu.make_async_copy(dec_out, w_do, load_sem.at[4]),
        pltpu.make_async_copy(expand, w_ex, load_sem.at[5]),
        pltpu.make_async_copy(shrink, w_sh, load_sem.at[6]),
    ]
    barrier = pltpu.get_barrier_semaphore()
    for peer in g_t.peers:
        pl.semaphore_signal(barrier, inc=1, device_id=(g_t.group, peer), device_id_type=MESH)
    for load in loads:
        load.start()

    me = g_t.me
    tb[me] = tokens[...]
    pl.semaphore_wait(barrier, len(g_t.peers))
    g_t.start()

    row_id = lax.broadcasted_iota(jnp.int32, (rows, rows), 0)
    col_id = lax.broadcasted_iota(jnp.int32, (rows, rows), 1)
    eye = row_id == col_id
    order_row = jnp.broadcast_to(order[...].astype(F32), (rows, rows))
    order_col = jnp.sum(jnp.where(eye, order_row, 0.0), axis=1, keepdims=True)
    seen_col = jnp.broadcast_to(order_col, (rows, rows)) < visible_count
    before = jnp.sum(jnp.where((row_id < col_id) & seen_col, 1.0, 0.0), axis=0, keepdims=True)
    before = jnp.broadcast_to(before, (rows, rows))
    slot = jnp.where(order_row < visible_count, before, vis + col_id.astype(F32) - before)
    to_slot = jnp.where(row_id.astype(F32) == slot, 1.0, 0.0)
    slot_col = jnp.sum(jnp.where(eye, slot, 0.0), axis=1, keepdims=True)
    from_slot = jnp.where(col_id.astype(F32) == slot_col, 1.0, 0.0).astype(BF)
    ranks = jnp.sum(to_slot * order_row, axis=1, keepdims=True)[:vis].astype(jnp.int32)
    ranks = jnp.broadcast_to(ranks, (vis, 128))
    upper = lax.div(ranks, 16)
    lower = (ranks - upper * 16).astype(F32).astype(BF)
    upper = upper.astype(F32).astype(BF)

    pos_slot = matmul(to_slot.astype(BF), pos[...])
    dec_hid = (pos_slot[vis:] + mask[...].astype(F32).reshape(1, -1)).astype(BF)
    loads[0].wait()
    act_hid = matmul(normalize(dec_hid), w_dec[...]).astype(BF)
    xb[me, 0:vis, :] = pos_slot[:vis].astype(BF)
    xb[me, vis:rows, :] = act_hid[:, dec_width:]
    half = vis // 2
    xb[me, rows : rows + half, 0:128] = upper[:half]
    xb[me, rows : rows + half, 128:256] = upper[half:]
    xb[me, rows : rows + half, 256:384] = lower[:half]
    xb[me, rows : rows + half, 384:512] = lower[half:]
    g_x.push(me, g_x.x_peer)
    g_x.push(me, g_x.line[1])

    def pairs_of(blocks):
        rows_in = jnp.concatenate([tb[block] for block in blocks], axis=0)
        return matmul(normalize(rows_in), w_enc[:, enc_width:]).astype(BF)

    loads[1].wait()
    enc_q = spread_heads(matmul(normalize(tokens[...]), w_enc[:, :enc_width]).astype(BF), EH)
    dec_qh = spread_heads(act_hid[:, :dec_width], DH)

    g_t.forward()
    g_x.push(me, g_x.line[2])
    g_x.push(me, g_x.core_peer)
    pairs = [pairs_of(g_t.line)]
    g_t.forward_x()
    g_x.push(me, g_x.line[3])
    pairs.append(pairs_of(g_t.line_x))
    g_x.forward((1,))
    g_t.finish()
    pairs.append(pairs_of(g_t.other))
    g_x.forward((2,))
    pairs = jnp.concatenate(pairs, axis=0)
    scores = matmul_nt(enc_q, pairs[:, :enc_width])
    _, powers, total = softmax_part(scores, (enc_width // EH) ** (-0.5) * LOG2E)
    g_x.forward((3,))
    mix = gather_heads(matmul(powers, pairs[:, enc_width:]) / total, EH)
    loads[2].wait()
    latent = (tokens[...].astype(F32) + matmul(mix, w_eo[...])).astype(BF)
    latent_out[...] = latent
    loads[3].wait()
    eb[me] = matmul(normalize(latent), w_emb[...]).astype(BF)
    g_e.start()

    g_x.forward_x()
    g_e.forward()
    g_x.finish()
    factor = (dec_width // DH) ** (-0.5) * LOG2E
    hid_keys = xb[:, vis:rows, 0:dec_width].reshape(peers * hid, dec_width)
    hid_values = xb[:, vis:rows, dec_width : 2 * dec_width].reshape(peers * hid, dec_width)
    middle_row = dec_qh.shape[0] // 2
    parts = []
    for queries in (dec_qh[:middle_row], dec_qh[middle_row:]):
        top, powers, total = softmax_part(matmul_nt(queries, hid_keys), factor)
        parts.append((top, total, matmul(powers, hid_values)))
        if len(parts) == 1:
            g_e.forward_x()
    top_hh, sum_hh, acc_hh = (jnp.concatenate(pair, axis=0) for pair in zip(*parts))

    g_e.finish()
    rank_hi = jnp.concatenate(
        [xb[:, rows : rows + half, 0:128].astype(F32), xb[:, rows : rows + half, 128:256].astype(F32)], axis=1
    ).reshape(visible_count, 128)
    rank_lo = jnp.concatenate(
        [xb[:, rows : rows + half, 256:384].astype(F32), xb[:, rows : rows + half, 384:512].astype(F32)], axis=1
    ).reshape(visible_count, 128)
    rank = rank_hi * 16.0 + rank_lo
    lane = lax.broadcasted_iota(jnp.int32, (visible_count, 128), 1).astype(F32)
    hot = jnp.concatenate(
        [jnp.where(rank == lane + 128.0 * k, 1.0, 0.0).astype(BF) for k in range(visible_count // 128)], axis=1
    )
    width = eb.shape[2]
    picked = matmul(hot, eb[...].reshape(visible_count, width))
    dec_vis = (picked + xb[:, 0:vis, :].reshape(visible_count, width).astype(F32)).astype(BF)
    din[...] = dec_vis.reshape(peers, vis, width)
    pairs_vis = matmul(normalize(dec_vis), w_dec[:, dec_width:]).astype(BF)
    own_vis = din[me]
    dec_qv = spread_heads(matmul(normalize(own_vis), w_dec[:, :dec_width]).astype(BF), DH)
    vis_keys, vis_values = pairs_vis[:, :dec_width], pairs_vis[:, dec_width:]

    def merge(scores, top, total, acc):
        highest = jnp.maximum(top, jnp.max(scores, -1, keepdims=True))
        powers = jnp.exp2((scores - highest) * factor)
        fade = jnp.exp2((top - highest) * factor)
        total = total * fade + jnp.sum(powers, -1, keepdims=True)
        return (acc * fade + matmul(powers.astype(BF), vis_values)) / total

    mix_h = gather_heads(merge(matmul_nt(dec_qh, vis_keys), top_hh, sum_hh, acc_hh), DH)
    top_vh, pow_vh, sum_vh = softmax_part(matmul_nt(dec_qv, hid_keys), factor)
    acc_vh = matmul(pow_vh, hid_values)
    mix_v = gather_heads(merge(matmul_nt(dec_qv, vis_keys), top_vh, sum_vh, acc_vh), DH)

    dec_in = jnp.concatenate([own_vis, dec_hid], axis=0)
    dec_mix = jnp.concatenate([mix_v, mix_h], axis=0)
    loads[4].wait()
    middle = (dec_in.astype(F32) + matmul(dec_mix, w_do[...])).astype(BF)
    loads[5].wait()
    wide = matmul(normalize(middle), w_ex[...])
    hidden = (0.5 * wide * (1.0 + erf(wide * 0.7071067811865476))).astype(BF)
    loads[6].wait()
    decoded = (middle.astype(F32) + matmul(hidden, w_sh[...])).astype(BF)
    decoded_out[...] = matmul(from_slot, decoded).astype(BF)
    g_t.sent()
    g_x.sent()
    g_e.sent()


def hand_out(latent, decoded, latent_out, decoded_out, sem):
    copies = [
        pltpu.make_async_copy(latent, latent_out, sem.at[0]),
        pltpu.make_async_copy(decoded, decoded_out, sem.at[1]),
    ]
    for copy in copies:
        copy.start()
    for copy in copies:
        copy.wait()


def on_device(peers, tokens, order, enc_proj, enc_out, embed, mask, pos, dec_proj, dec_out, expand, shrink):
    vis, rows, width = tokens.shape[0], pos.shape[0], pos.shape[1]
    weights = (enc_proj, enc_out, embed, dec_proj, dec_out, expand, shrink)
    vmem = pl.BlockSpec(memory_space=pltpu.VMEM)
    anywhere = pl.BlockSpec(memory_space=pl.ANY)
    latent, decoded = pl.pallas_call(
        kernel,
        out_shape=(
            jax.ShapeDtypeStruct(tokens.shape, BF),
            jax.ShapeDtypeStruct(pos.shape, BF),
        ),
        in_specs=[vmem, vmem, anywhere, anywhere, anywhere, vmem, vmem, anywhere, anywhere, anywhere, anywhere],
        out_specs=(vmem, vmem),
        scratch_shapes=[pltpu.VMEM(w.shape, BF) for w in weights]
        + [
            pltpu.VMEM((peers, vis, tokens.shape[1]), BF),
            pltpu.VMEM((peers, rows + vis // 2, width), BF),
            pltpu.VMEM((peers, vis, width), BF),
            pltpu.VMEM((peers, vis, width), BF),
            pltpu.SemaphoreType.DMA((7,)),
        ]
        + [pltpu.SemaphoreType.DMA((n,)) for _ in range(3) for n in (15, peers)],
        compiler_params=pltpu.CompilerParams(
            collective_id=0, has_side_effects=True, vmem_limit_bytes=56 * 1024 * 1024
        ),
    )(tokens, order.reshape(1, rows), enc_proj, enc_out, embed, mask, pos,
      dec_proj, dec_out, expand, shrink)
    return pl.pallas_call(
        hand_out,
        out_shape=(jax.ShapeDtypeStruct(tokens.shape, BF), jax.ShapeDtypeStruct(pos.shape, BF)),
        in_specs=[anywhere, anywhere],
        out_specs=(anywhere, anywhere),
        scratch_shapes=[pltpu.SemaphoreType.DMA((2,))],
    )(latent, decoded)


def solution(mesh):
    in_specs = (
        P(("groups", "seq"), None),
        P(("groups", "seq")),
        P(),
        P(),
        P(),
        P(),
        P("seq", None),
        P(),
        P(),
        P(),
        P(),
    )
    out_specs = (P(("groups", "seq"), None), P(("groups", "seq"), None))
    peers = mesh.shape["seq"]
    body = functools.partial(on_device, peers) if peers == 16 else on_device_plain
    return jax.shard_map(
        body, mesh=mesh, in_specs=in_specs, out_specs=out_specs, check_vma=False
    )
```

```python
import functools

import jax
import jax.numpy as jnp
from jax import lax
from jax.experimental import pallas as pl
from jax.experimental.pallas import tpu as pltpu
from jax.sharding import PartitionSpec as P

EH = 8
DH = 8


def normalize(values):
    values = values.astype(jnp.float32)
    centre = values - jnp.mean(values, -1, keepdims=True)
    spread = jnp.mean(centre * centre, -1, keepdims=True)
    return (centre * lax.rsqrt(spread + 1e-06)).astype(jnp.bfloat16)


def attend(queries, keys, values, heads):
    total, width = queries.shape
    size = width // heads
    query_heads = queries.reshape(total, heads, size).transpose(1, 0, 2)
    key_heads = keys.reshape(keys.shape[0], heads, size).transpose(1, 0, 2)
    value_heads = values.reshape(values.shape[0], heads, size).transpose(1, 0, 2)

    def one_head(operands):
        query_part, key_part, value_part = operands
        scores = lax.dot_general(
            query_part, key_part, (((1,), (1,)), ((), ())), preferred_element_type=jnp.float32
        ) * size ** (-0.5)
        highest = jnp.max(scores, -1, keepdims=True)
        powers = jnp.exp(scores - highest)
        weights = (powers / jnp.sum(powers, -1, keepdims=True)).astype(jnp.bfloat16)
        return jnp.dot(weights, value_part, preferred_element_type=jnp.float32).astype(jnp.bfloat16)

    result = lax.map(one_head, (query_heads, key_heads, value_heads))
    return result.transpose(1, 0, 2).reshape(total, width)


def on_device_plain(
    visible_tokens,
    restore_order,
    encoder_project,
    encoder_output,
    decoder_embed,
    mask_token,
    position_table,
    decoder_project,
    decoder_output,
    expand_weight,
    shrink_weight,
):
    enc_width = encoder_output.shape[0]
    dec_width = decoder_output.shape[0]
    enc_act = jnp.dot(
        normalize(visible_tokens), encoder_project, preferred_element_type=jnp.float32
    ).astype(jnp.bfloat16)
    enc_pairs = lax.all_gather(enc_act[:, enc_width:], "seq", axis=0, tiled=True)
    enc_mix = attend(enc_act[:, :enc_width], enc_pairs[:, :enc_width], enc_pairs[:, enc_width:], EH)
    latent = (
        visible_tokens.astype(jnp.float32)
        + jnp.dot(enc_mix, encoder_output, preferred_element_type=jnp.float32)
    ).astype(jnp.bfloat16)
    peers = lax.axis_size("seq")
    vis_rows = latent.shape[0]
    visible_count = vis_rows * peers
    seen = restore_order < visible_count
    chosen = jnp.minimum(restore_order, visible_count - 1)
    local_embedded = jnp.dot(
        normalize(latent), decoder_embed, preferred_element_type=jnp.float32
    ).astype(jnp.bfloat16)
    capacity = max(1, vis_rows // peers)
    owners = chosen // vis_rows
    offsets = chosen % vis_rows
    owner_hot = (
        (owners[:, None] == jnp.arange(peers, dtype=jnp.int32)[None, :]) & seen[:, None]
    ).astype(jnp.int32)
    earlier = jnp.cumsum(owner_hot, axis=0) - owner_hot
    slot_index = jnp.sum(earlier * owner_hot, axis=1)
    flat_slot = owners * capacity + slot_index
    target_hot = (
        flat_slot[:, None] == jnp.arange(peers * capacity, dtype=jnp.int32)[None, :]
    ) & seen[:, None]
    requests = jnp.max(jnp.where(target_hot, offsets[:, None], -1), axis=0).reshape(peers, capacity)
    asked = lax.all_to_all(requests, "seq", split_axis=0, concat_axis=0, tiled=True)
    answers = jnp.take(local_embedded, jnp.maximum(asked, 0).reshape(-1), axis=0).reshape(
        peers, capacity, local_embedded.shape[1]
    )
    replies = lax.all_to_all(answers, "seq", split_axis=0, concat_axis=0, tiled=True)
    replies = replies.reshape(peers * capacity, local_embedded.shape[1])
    picked = jnp.take(replies, jnp.minimum(flat_slot, peers * capacity - 1), axis=0)
    filled = jnp.where(
        seen[:, None], picked.astype(jnp.float32), mask_token.astype(jnp.float32)[None, :]
    )
    dec_in = (filled + position_table.astype(jnp.float32)).astype(jnp.bfloat16)
    dec_act = jnp.dot(
        normalize(dec_in), decoder_project, preferred_element_type=jnp.float32
    ).astype(jnp.bfloat16)
    dec_pairs = lax.all_gather(dec_act[:, dec_width:], "seq", axis=0, tiled=True)
    dec_mix = attend(dec_act[:, :dec_width], dec_pairs[:, :dec_width], dec_pairs[:, dec_width:], DH)
    middle = (
        dec_in.astype(jnp.float32)
        + jnp.dot(dec_mix, decoder_output, preferred_element_type=jnp.float32)
    ).astype(jnp.bfloat16)
    hidden = jax.nn.gelu(
        jnp.dot(normalize(middle), expand_weight, preferred_element_type=jnp.float32),
        approximate=False,
    ).astype(jnp.bfloat16)
    decoded = (
        middle.astype(jnp.float32)
        + jnp.dot(hidden, shrink_weight, preferred_element_type=jnp.float32)
    ).astype(jnp.bfloat16)
    return (latent, decoded)


BF = jnp.bfloat16
F32 = jnp.float32
MESH = pl.DeviceIdType.MESH
LOG2E = 1.4426950408889634


def matmul(left, right):
    return jnp.dot(left, right, preferred_element_type=F32)


def matmul_nt(left, right):
    return lax.dot_general(left, right, (((1,), (1,)), ((), ())), preferred_element_type=F32)


def erf(value):
    value = jnp.clip(value, -3.832506856900711, 3.832506856900711)
    square = value * value
    top = jnp.full_like(value, 0.00022905065861350646)
    for coef in (0.0034082910107109506, 0.050955695062380861, 0.18520832239976145, 1.128379143519084):
        top = top * square + coef
    low = jnp.full_like(value, -1.1791602954361697e-7)
    for coef in (
        0.000023547966471313185,
        0.0010179625278914885,
        0.014070470171167667,
        0.11098505178285362,
        0.49746925110067538,
        1.0,
    ):
        low = low * square + coef
    return value * top / low


def lane_heads(rows, width, heads):
    lane = lax.broadcasted_iota(jnp.int32, (rows, width), 1)
    size = width // heads
    return [(lane >= h * size) & (lane < (h + 1) * size) for h in range(heads)]


def spread_heads(queries, heads):
    wide = queries.astype(F32)
    masks = lane_heads(*queries.shape, heads)
    return jnp.concatenate([jnp.where(mask, wide, 0.0).astype(BF) for mask in masks], axis=0)


def gather_heads(stacked, heads):
    rows, width = stacked.shape[0] // heads, stacked.shape[1]
    masks = lane_heads(rows, width, heads)
    total = jnp.zeros((rows, width), F32)
    for h, mask in enumerate(masks):
        total = jnp.where(mask, stacked[h * rows : (h + 1) * rows], total)
    return total.astype(BF)


class Gather:
    def __init__(self, buf, send, recv):
        self.buf, self.send, self.recv = buf, send, recv
        me = lax.axis_index("seq")
        self.group = lax.axis_index("groups")
        core = lax.rem(me, 2)
        x = lax.rem(lax.div(me, 2), 2)
        low = lax.rem(lax.div(me, 4), 2)
        high = lax.div(me, 8)

        def place(flip_high, flip_low, flip_x, flip_core):
            a = 1 - high if flip_high else high
            b = 1 - low if flip_low else low
            c = 1 - x if flip_x else x
            d = 1 - core if flip_core else core
            return a * 8 + b * 4 + c * 2 + d

        self.line = [place(k // 2, k % 2, 0, 0) for k in range(4)]
        self.line_x = [place(k // 2, k % 2, 1, 0) for k in range(4)]
        self.other = [place(k // 2, k % 2, q, 1) for q in range(2) for k in range(4)]
        self.me, self.x_peer, self.core_peer = me, self.line_x[0], self.other[0]
        self.peers = self.line[1:] + [self.x_peer, self.core_peer]
        self.started = []

    def copy(self, block, slot, peer):
        return pltpu.make_async_remote_copy(
            src_ref=self.buf.at[block],
            dst_ref=self.buf.at[block],
            send_sem=self.send.at[slot],
            recv_sem=self.recv.at[block],
            device_id=(self.group, peer),
            device_id_type=MESH,
        )

    def push(self, block, peer):
        copy = self.copy(block, len(self.started), peer)
        copy.start()
        self.started.append(copy)

    def arrive(self, block):
        self.copy(block, 0, self.core_peer).wait_recv()

    def start(self):
        for k in (3, 2, 1):
            self.push(self.me, self.line[k])
        self.push(self.me, self.x_peer)
        self.push(self.me, self.core_peer)

    def forward(self, steps=(1, 2, 3)):
        for k in steps:
            self.arrive(self.line[k])
            self.push(self.line[k], self.x_peer)
            self.push(self.line[k], self.core_peer)

    def forward_x(self):
        for k in range(4):
            self.arrive(self.line_x[k])
            self.push(self.line_x[k], self.core_peer)

    def finish(self):
        for block in self.other:
            self.arrive(block)

    def sent(self):
        for copy in self.started:
            copy.wait_send()


def softmax_part(scores, factor):
    highest = jnp.max(scores, -1, keepdims=True)
    powers = jnp.exp2((scores - highest) * factor)
    return highest, powers.astype(BF), jnp.sum(powers, -1, keepdims=True)


def kernel(
    tokens, order, enc_proj, enc_out, embed, mask, pos, dec_proj, dec_out, expand, shrink,
    latent_out, decoded_out,
    w_enc, w_eo, w_emb, w_dec, w_do, w_ex, w_sh,
    tb, xb, eb, din, load_sem,
    t_send, t_recv, x_send, x_recv, e_send, e_recv,
):
    peers, vis, _ = tb.shape
    enc_width = w_eo.shape[0]
    enc2 = 2 * enc_width
    dec_width = w_do.shape[0]
    rows = pos.shape[0]
    hid = rows - vis
    visible_count = peers * vis

    g_t = Gather(tb, t_send, t_recv)
    g_x = Gather(xb, x_send, x_recv)
    g_e = Gather(eb, e_send, e_recv)

    loads = [
        pltpu.make_async_copy(dec_proj, w_dec, load_sem.at[0]),
        pltpu.make_async_copy(enc_proj, w_enc, load_sem.at[1]),
        pltpu.make_async_copy(enc_out, w_eo, load_sem.at[2]),
        pltpu.make_async_copy(embed, w_emb, load_sem.at[3]),
        pltpu.make_async_copy(dec_out, w_do, load_sem.at[4]),
        pltpu.make_async_copy(expand, w_ex, load_sem.at[5]),
        pltpu.make_async_copy(shrink, w_sh, load_sem.at[6]),
    ]
    barrier = pltpu.get_barrier_semaphore()
    for peer in g_t.peers:
        pl.semaphore_signal(barrier, inc=1, device_id=(g_t.group, peer), device_id_type=MESH)
    for load in loads:
        load.start()

    me = g_t.me
    tb[me] = tokens[...]
    pl.semaphore_wait(barrier, len(g_t.peers))
    g_t.start()

    row_id = lax.broadcasted_iota(jnp.int32, (rows, rows), 0)
    col_id = lax.broadcasted_iota(jnp.int32, (rows, rows), 1)
    eye = row_id == col_id
    order_row = jnp.broadcast_to(order[...].astype(F32), (rows, rows))
    order_col = jnp.sum(jnp.where(eye, order_row, 0.0), axis=1, keepdims=True)
    seen_col = jnp.broadcast_to(order_col, (rows, rows)) < visible_count
    before = jnp.sum(jnp.where((row_id < col_id) & seen_col, 1.0, 0.0), axis=0, keepdims=True)
    before = jnp.broadcast_to(before, (rows, rows))
    slot = jnp.where(order_row < visible_count, before, vis + col_id.astype(F32) - before)
    to_slot = jnp.where(row_id.astype(F32) == slot, 1.0, 0.0)
    slot_col = jnp.sum(jnp.where(eye, slot, 0.0), axis=1, keepdims=True)
    from_slot = jnp.where(col_id.astype(F32) == slot_col, 1.0, 0.0).astype(BF)
    ranks = jnp.sum(to_slot * order_row, axis=1, keepdims=True)[:vis].astype(jnp.int32)
    ranks = jnp.broadcast_to(ranks, (vis, 128))
    upper = lax.div(ranks, 16)
    lower = (ranks - upper * 16).astype(F32).astype(BF)
    upper = upper.astype(F32).astype(BF)

    pos_slot = matmul(to_slot.astype(BF), pos[...])
    dec_hid = (pos_slot[vis:] + mask[...].astype(F32).reshape(1, -1)).astype(BF)
    loads[0].wait()
    act_hid = matmul(normalize(dec_hid), w_dec[...]).astype(BF)
    xb[me, 0:vis, :] = pos_slot[:vis].astype(BF)
    xb[me, vis:rows, :] = act_hid[:, dec_width:]
    half = vis // 2
    xb[me, rows : rows + half, 0:128] = upper[:half]
    xb[me, rows : rows + half, 128:256] = upper[half:]
    xb[me, rows : rows + half, 256:384] = lower[:half]
    xb[me, rows : rows + half, 384:512] = lower[half:]
    g_x.push(me, g_x.x_peer)
    g_x.push(me, g_x.line[1])

    def pairs_of(blocks):
        rows_in = jnp.concatenate([tb[block] for block in blocks], axis=0)
        return matmul(normalize(rows_in), w_enc[:, enc_width:]).astype(BF)

    loads[1].wait()
    enc_q = spread_heads(matmul(normalize(tokens[...]), w_enc[:, :enc_width]).astype(BF), EH)
    dec_qh = spread_heads(act_hid[:, :dec_width], DH)

    g_t.forward()
    g_x.push(me, g_x.line[2])
    g_x.push(me, g_x.core_peer)
    pairs = [pairs_of(g_t.line)]
    g_t.forward_x()
    g_x.push(me, g_x.line[3])
    pairs.append(pairs_of(g_t.line_x))
    g_x.forward((1,))
    g_t.finish()
    pairs.append(pairs_of(g_t.other))
    g_x.forward((2,))
    pairs = jnp.concatenate(pairs, axis=0)
    scores = matmul_nt(enc_q, pairs[:, :enc_width])
    _, powers, total = softmax_part(scores, (enc_width // EH) ** (-0.5) * LOG2E)
    mix = gather_heads(matmul(powers, pairs[:, enc_width:]) / total, EH)
    loads[2].wait()
    latent = (tokens[...].astype(F32) + matmul(mix, w_eo[...])).astype(BF)
    latent_out[...] = latent
    loads[3].wait()
    eb[me] = matmul(normalize(latent), w_emb[...]).astype(BF)
    g_e.start()

    g_x.forward((3,))
    g_e.forward()
    g_x.forward_x()
    g_x.finish()
    factor = (dec_width // DH) ** (-0.5) * LOG2E
    hid_keys = xb[:, vis:rows, 0:dec_width].reshape(peers * hid, dec_width)
    hid_values = xb[:, vis:rows, dec_width : 2 * dec_width].reshape(peers * hid, dec_width)
    middle_row = dec_qh.shape[0] // 2
    parts = []
    for queries in (dec_qh[:middle_row], dec_qh[middle_row:]):
        top, powers, total = softmax_part(matmul_nt(queries, hid_keys), factor)
        parts.append((top, total, matmul(powers, hid_values)))
        if len(parts) == 1:
            g_e.forward_x()
    top_hh, sum_hh, acc_hh = (jnp.concatenate(pair, axis=0) for pair in zip(*parts))

    g_e.finish()
    rank_hi = jnp.concatenate(
        [xb[:, rows : rows + half, 0:128].astype(F32), xb[:, rows : rows + half, 128:256].astype(F32)], axis=1
    ).reshape(visible_count, 128)
    rank_lo = jnp.concatenate(
        [xb[:, rows : rows + half, 256:384].astype(F32), xb[:, rows : rows + half, 384:512].astype(F32)], axis=1
    ).reshape(visible_count, 128)
    rank = rank_hi * 16.0 + rank_lo
    lane = lax.broadcasted_iota(jnp.int32, (visible_count, 128), 1).astype(F32)
    hot = jnp.concatenate(
        [jnp.where(rank == lane + 128.0 * k, 1.0, 0.0).astype(BF) for k in range(visible_count // 128)], axis=1
    )
    width = eb.shape[2]
    picked = matmul(hot, eb[...].reshape(visible_count, width))
    dec_vis = (picked + xb[:, 0:vis, :].reshape(visible_count, width).astype(F32)).astype(BF)
    din[...] = dec_vis.reshape(peers, vis, width)
    pairs_vis = matmul(normalize(dec_vis), w_dec[:, dec_width:]).astype(BF)
    own_vis = din[me]
    dec_qv = spread_heads(matmul(normalize(own_vis), w_dec[:, :dec_width]).astype(BF), DH)
    vis_keys, vis_values = pairs_vis[:, :dec_width], pairs_vis[:, dec_width:]

    def merge(scores, top, total, acc):
        highest = jnp.maximum(top, jnp.max(scores, -1, keepdims=True))
        powers = jnp.exp2((scores - highest) * factor)
        fade = jnp.exp2((top - highest) * factor)
        total = total * fade + jnp.sum(powers, -1, keepdims=True)
        return (acc * fade + matmul(powers.astype(BF), vis_values)) / total

    mix_h = gather_heads(merge(matmul_nt(dec_qh, vis_keys), top_hh, sum_hh, acc_hh), DH)
    top_vh, pow_vh, sum_vh = softmax_part(matmul_nt(dec_qv, hid_keys), factor)
    acc_vh = matmul(pow_vh, hid_values)
    mix_v = gather_heads(merge(matmul_nt(dec_qv, vis_keys), top_vh, sum_vh, acc_vh), DH)

    dec_in = jnp.concatenate([own_vis, dec_hid], axis=0)
    dec_mix = jnp.concatenate([mix_v, mix_h], axis=0)
    loads[4].wait()
    middle = (dec_in.astype(F32) + matmul(dec_mix, w_do[...])).astype(BF)
    loads[5].wait()
    wide = matmul(normalize(middle), w_ex[...])
    hidden = (0.5 * wide * (1.0 + erf(wide * 0.7071067811865476))).astype(BF)
    loads[6].wait()
    decoded = (middle.astype(F32) + matmul(hidden, w_sh[...])).astype(BF)
    decoded_out[...] = matmul(from_slot, decoded).astype(BF)
    g_t.sent()
    g_x.sent()
    g_e.sent()


def on_device(peers, tokens, order, enc_proj, enc_out, embed, mask, pos, dec_proj, dec_out, expand, shrink):
    vis, rows, width = tokens.shape[0], pos.shape[0], pos.shape[1]
    weights = (enc_proj, enc_out, embed, dec_proj, dec_out, expand, shrink)
    vmem = pl.BlockSpec(memory_space=pltpu.VMEM)
    anywhere = pl.BlockSpec(memory_space=pl.ANY)
    latent, decoded = pl.pallas_call(
        kernel,
        out_shape=(
            jax.ShapeDtypeStruct(tokens.shape, BF),
            jax.ShapeDtypeStruct(pos.shape, BF),
        ),
        in_specs=[vmem, vmem, anywhere, anywhere, anywhere, vmem, vmem, anywhere, anywhere, anywhere, anywhere],
        out_specs=(vmem, vmem),
        scratch_shapes=[pltpu.VMEM(w.shape, BF) for w in weights]
        + [
            pltpu.VMEM((peers, vis, tokens.shape[1]), BF),
            pltpu.VMEM((peers, rows + vis // 2, width), BF),
            pltpu.VMEM((peers, vis, width), BF),
            pltpu.VMEM((peers, vis, width), BF),
            pltpu.SemaphoreType.DMA((7,)),
        ]
        + [pltpu.SemaphoreType.DMA((n,)) for _ in range(3) for n in (15, peers)],
        compiler_params=pltpu.CompilerParams(
            collective_id=0, has_side_effects=True, vmem_limit_bytes=56 * 1024 * 1024
        ),
    )(tokens, order.reshape(1, rows), enc_proj, enc_out, embed, mask, pos,
      dec_proj, dec_out, expand, shrink)
    return latent, decoded


def solution(mesh):
    in_specs = (
        P(("groups", "seq"), None),
        P(("groups", "seq")),
        P(),
        P(),
        P(),
        P(),
        P("seq", None),
        P(),
        P(),
        P(),
        P(),
    )
    out_specs = (P(("groups", "seq"), None), P(("groups", "seq"), None))
    peers = mesh.shape["seq"]
    body = functools.partial(on_device, peers) if peers == 16 else on_device_plain
    return jax.shard_map(
        body, mesh=mesh, in_specs=in_specs, out_specs=out_specs, check_vma=False
    )
```

```python
import functools

import jax
import jax.numpy as jnp
from jax import lax
from jax.experimental import pallas as pl
from jax.experimental.pallas import tpu as pltpu
from jax.sharding import PartitionSpec as P

EH = 8
DH = 8


def normalize(values):
    values = values.astype(jnp.float32)
    centre = values - jnp.mean(values, -1, keepdims=True)
    spread = jnp.mean(centre * centre, -1, keepdims=True)
    return (centre * lax.rsqrt(spread + 1e-06)).astype(jnp.bfloat16)


def attend(queries, keys, values, heads):
    total, width = queries.shape
    size = width // heads
    query_heads = queries.reshape(total, heads, size).transpose(1, 0, 2)
    key_heads = keys.reshape(keys.shape[0], heads, size).transpose(1, 0, 2)
    value_heads = values.reshape(values.shape[0], heads, size).transpose(1, 0, 2)

    def one_head(operands):
        query_part, key_part, value_part = operands
        scores = lax.dot_general(
            query_part, key_part, (((1,), (1,)), ((), ())), preferred_element_type=jnp.float32
        ) * size ** (-0.5)
        highest = jnp.max(scores, -1, keepdims=True)
        powers = jnp.exp(scores - highest)
        weights = (powers / jnp.sum(powers, -1, keepdims=True)).astype(jnp.bfloat16)
        return jnp.dot(weights, value_part, preferred_element_type=jnp.float32).astype(jnp.bfloat16)

    result = lax.map(one_head, (query_heads, key_heads, value_heads))
    return result.transpose(1, 0, 2).reshape(total, width)


def on_device_plain(
    visible_tokens,
    restore_order,
    encoder_project,
    encoder_output,
    decoder_embed,
    mask_token,
    position_table,
    decoder_project,
    decoder_output,
    expand_weight,
    shrink_weight,
):
    enc_width = encoder_output.shape[0]
    dec_width = decoder_output.shape[0]
    enc_act = jnp.dot(
        normalize(visible_tokens), encoder_project, preferred_element_type=jnp.float32
    ).astype(jnp.bfloat16)
    enc_pairs = lax.all_gather(enc_act[:, enc_width:], "seq", axis=0, tiled=True)
    enc_mix = attend(enc_act[:, :enc_width], enc_pairs[:, :enc_width], enc_pairs[:, enc_width:], EH)
    latent = (
        visible_tokens.astype(jnp.float32)
        + jnp.dot(enc_mix, encoder_output, preferred_element_type=jnp.float32)
    ).astype(jnp.bfloat16)
    peers = lax.axis_size("seq")
    vis_rows = latent.shape[0]
    visible_count = vis_rows * peers
    seen = restore_order < visible_count
    chosen = jnp.minimum(restore_order, visible_count - 1)
    local_embedded = jnp.dot(
        normalize(latent), decoder_embed, preferred_element_type=jnp.float32
    ).astype(jnp.bfloat16)
    capacity = max(1, vis_rows // peers)
    owners = chosen // vis_rows
    offsets = chosen % vis_rows
    owner_hot = (
        (owners[:, None] == jnp.arange(peers, dtype=jnp.int32)[None, :]) & seen[:, None]
    ).astype(jnp.int32)
    earlier = jnp.cumsum(owner_hot, axis=0) - owner_hot
    slot_index = jnp.sum(earlier * owner_hot, axis=1)
    flat_slot = owners * capacity + slot_index
    target_hot = (
        flat_slot[:, None] == jnp.arange(peers * capacity, dtype=jnp.int32)[None, :]
    ) & seen[:, None]
    requests = jnp.max(jnp.where(target_hot, offsets[:, None], -1), axis=0).reshape(peers, capacity)
    asked = lax.all_to_all(requests, "seq", split_axis=0, concat_axis=0, tiled=True)
    answers = jnp.take(local_embedded, jnp.maximum(asked, 0).reshape(-1), axis=0).reshape(
        peers, capacity, local_embedded.shape[1]
    )
    replies = lax.all_to_all(answers, "seq", split_axis=0, concat_axis=0, tiled=True)
    replies = replies.reshape(peers * capacity, local_embedded.shape[1])
    picked = jnp.take(replies, jnp.minimum(flat_slot, peers * capacity - 1), axis=0)
    filled = jnp.where(
        seen[:, None], picked.astype(jnp.float32), mask_token.astype(jnp.float32)[None, :]
    )
    dec_in = (filled + position_table.astype(jnp.float32)).astype(jnp.bfloat16)
    dec_act = jnp.dot(
        normalize(dec_in), decoder_project, preferred_element_type=jnp.float32
    ).astype(jnp.bfloat16)
    dec_pairs = lax.all_gather(dec_act[:, dec_width:], "seq", axis=0, tiled=True)
    dec_mix = attend(dec_act[:, :dec_width], dec_pairs[:, :dec_width], dec_pairs[:, dec_width:], DH)
    middle = (
        dec_in.astype(jnp.float32)
        + jnp.dot(dec_mix, decoder_output, preferred_element_type=jnp.float32)
    ).astype(jnp.bfloat16)
    hidden = jax.nn.gelu(
        jnp.dot(normalize(middle), expand_weight, preferred_element_type=jnp.float32),
        approximate=False,
    ).astype(jnp.bfloat16)
    decoded = (
        middle.astype(jnp.float32)
        + jnp.dot(hidden, shrink_weight, preferred_element_type=jnp.float32)
    ).astype(jnp.bfloat16)
    return (latent, decoded)


BF = jnp.bfloat16
F32 = jnp.float32
MESH = pl.DeviceIdType.MESH
LOG2E = 1.4426950408889634


def matmul(left, right):
    return jnp.dot(left, right, preferred_element_type=F32)


def matmul_nt(left, right):
    return lax.dot_general(left, right, (((1,), (1,)), ((), ())), preferred_element_type=F32)


def erf(value):
    value = jnp.clip(value, -3.832506856900711, 3.832506856900711)
    square = value * value
    top = jnp.full_like(value, 0.00022905065861350646)
    for coef in (0.0034082910107109506, 0.050955695062380861, 0.18520832239976145, 1.128379143519084):
        top = top * square + coef
    low = jnp.full_like(value, -1.1791602954361697e-7)
    for coef in (
        0.000023547966471313185,
        0.0010179625278914885,
        0.014070470171167667,
        0.11098505178285362,
        0.49746925110067538,
        1.0,
    ):
        low = low * square + coef
    return value * top / low


def lane_heads(rows, width, heads):
    lane = lax.broadcasted_iota(jnp.int32, (rows, width), 1)
    size = width // heads
    return [(lane >= h * size) & (lane < (h + 1) * size) for h in range(heads)]


def spread_heads(queries, heads):
    wide = queries.astype(F32)
    masks = lane_heads(*queries.shape, heads)
    return jnp.concatenate([jnp.where(mask, wide, 0.0).astype(BF) for mask in masks], axis=0)


def gather_heads(stacked, heads):
    rows, width = stacked.shape[0] // heads, stacked.shape[1]
    masks = lane_heads(rows, width, heads)
    total = jnp.zeros((rows, width), F32)
    for h, mask in enumerate(masks):
        total = jnp.where(mask, stacked[h * rows : (h + 1) * rows], total)
    return total.astype(BF)


class Gather:
    def __init__(self, buf, send, recv):
        self.buf, self.send, self.recv = buf, send, recv
        me = lax.axis_index("seq")
        self.group = lax.axis_index("groups")
        core = lax.rem(me, 2)
        x = lax.rem(lax.div(me, 2), 2)
        low = lax.rem(lax.div(me, 4), 2)
        high = lax.div(me, 8)

        def place(flip_high, flip_low, flip_x, flip_core):
            a = 1 - high if flip_high else high
            b = 1 - low if flip_low else low
            c = 1 - x if flip_x else x
            d = 1 - core if flip_core else core
            return a * 8 + b * 4 + c * 2 + d

        self.line = [place(k // 2, k % 2, 0, 0) for k in range(4)]
        self.line_x = [place(k // 2, k % 2, 1, 0) for k in range(4)]
        self.other = [place(k // 2, k % 2, q, 1) for q in range(2) for k in range(4)]
        self.me, self.x_peer, self.core_peer = me, self.line_x[0], self.other[0]
        self.peers = self.line[1:] + [self.x_peer, self.core_peer]
        self.started = []

    def copy(self, block, slot, peer):
        return pltpu.make_async_remote_copy(
            src_ref=self.buf.at[block],
            dst_ref=self.buf.at[block],
            send_sem=self.send.at[slot],
            recv_sem=self.recv.at[block],
            device_id=(self.group, peer),
            device_id_type=MESH,
        )

    def push(self, block, peer):
        copy = self.copy(block, len(self.started), peer)
        copy.start()
        self.started.append(copy)

    def arrive(self, block):
        self.copy(block, 0, self.core_peer).wait_recv()

    def start(self):
        self.push(self.me, self.x_peer)
        for k in (1, 2, 3):
            self.push(self.me, self.line[k])
        self.push(self.me, self.core_peer)

    def forward(self, steps=(1, 2, 3)):
        for k in steps:
            self.arrive(self.line[k])
            self.push(self.line[k], self.x_peer)
            self.push(self.line[k], self.core_peer)

    def forward_x(self):
        for k in range(4):
            self.arrive(self.line_x[k])
            self.push(self.line_x[k], self.core_peer)

    def finish(self):
        for block in self.other:
            self.arrive(block)

    def sent(self):
        for copy in self.started:
            copy.wait_send()


def softmax_part(scores, factor):
    highest = jnp.max(scores, -1, keepdims=True)
    powers = jnp.exp2((scores - highest) * factor)
    return highest, powers.astype(BF), jnp.sum(powers, -1, keepdims=True)


def kernel(
    tokens, order, enc_proj, enc_out, embed, mask, pos, dec_proj, dec_out, expand, shrink,
    latent_out, decoded_out,
    w_enc, w_eo, w_emb, w_dec, w_do, w_ex, w_sh,
    tb, xb, eb, din, load_sem,
    t_send, t_recv, x_send, x_recv, e_send, e_recv,
):
    peers, vis, _ = tb.shape
    enc_width = w_eo.shape[0]
    enc2 = 2 * enc_width
    dec_width = w_do.shape[0]
    rows = pos.shape[0]
    hid = rows - vis
    visible_count = peers * vis

    g_t = Gather(tb, t_send, t_recv)
    g_x = Gather(xb, x_send, x_recv)
    g_e = Gather(eb, e_send, e_recv)

    loads = [
        pltpu.make_async_copy(dec_proj, w_dec, load_sem.at[0]),
        pltpu.make_async_copy(enc_proj, w_enc, load_sem.at[1]),
        pltpu.make_async_copy(enc_out, w_eo, load_sem.at[2]),
        pltpu.make_async_copy(embed, w_emb, load_sem.at[3]),
        pltpu.make_async_copy(dec_out, w_do, load_sem.at[4]),
        pltpu.make_async_copy(expand, w_ex, load_sem.at[5]),
        pltpu.make_async_copy(shrink, w_sh, load_sem.at[6]),
    ]
    barrier = pltpu.get_barrier_semaphore()
    for peer in g_t.peers:
        pl.semaphore_signal(barrier, inc=1, device_id=(g_t.group, peer), device_id_type=MESH)
    for load in loads:
        load.start()

    me = g_t.me
    tb[me] = tokens[...]
    pl.semaphore_wait(barrier, len(g_t.peers))
    g_t.start()

    row_id = lax.broadcasted_iota(jnp.int32, (rows, rows), 0)
    col_id = lax.broadcasted_iota(jnp.int32, (rows, rows), 1)
    eye = row_id == col_id
    order_row = jnp.broadcast_to(order[...].astype(F32), (rows, rows))
    order_col = jnp.sum(jnp.where(eye, order_row, 0.0), axis=1, keepdims=True)
    seen_col = jnp.broadcast_to(order_col, (rows, rows)) < visible_count
    before = jnp.sum(jnp.where((row_id < col_id) & seen_col, 1.0, 0.0), axis=0, keepdims=True)
    before = jnp.broadcast_to(before, (rows, rows))
    slot = jnp.where(order_row < visible_count, before, vis + col_id.astype(F32) - before)
    to_slot = jnp.where(row_id.astype(F32) == slot, 1.0, 0.0)
    slot_col = jnp.sum(jnp.where(eye, slot, 0.0), axis=1, keepdims=True)
    from_slot = jnp.where(col_id.astype(F32) == slot_col, 1.0, 0.0).astype(BF)
    ranks = jnp.sum(to_slot * order_row, axis=1, keepdims=True)[:vis].astype(jnp.int32)
    ranks = jnp.broadcast_to(ranks, (vis, 128))
    upper = lax.div(ranks, 16)
    lower = (ranks - upper * 16).astype(F32).astype(BF)
    upper = upper.astype(F32).astype(BF)

    pos_slot = matmul(to_slot.astype(BF), pos[...])
    dec_hid = (pos_slot[vis:] + mask[...].astype(F32).reshape(1, -1)).astype(BF)
    loads[0].wait()
    act_hid = matmul(normalize(dec_hid), w_dec[...]).astype(BF)
    xb[me, 0:vis, :] = pos_slot[:vis].astype(BF)
    xb[me, vis:rows, :] = act_hid[:, dec_width:]
    half = vis // 2
    xb[me, rows : rows + half, 0:128] = upper[:half]
    xb[me, rows : rows + half, 128:256] = upper[half:]
    xb[me, rows : rows + half, 256:384] = lower[:half]
    xb[me, rows : rows + half, 384:512] = lower[half:]
    g_x.push(me, g_x.x_peer)
    g_x.push(me, g_x.line[1])

    def pairs_of(blocks):
        rows_in = jnp.concatenate([tb[block] for block in blocks], axis=0)
        return matmul(normalize(rows_in), w_enc[:, enc_width:]).astype(BF)

    loads[1].wait()
    enc_q = spread_heads(matmul(normalize(tokens[...]), w_enc[:, :enc_width]).astype(BF), EH)
    dec_qh = spread_heads(act_hid[:, :dec_width], DH)

    g_t.forward()
    g_x.push(me, g_x.line[2])
    g_x.push(me, g_x.core_peer)
    pairs = [pairs_of(g_t.line)]
    g_t.forward_x()
    g_x.push(me, g_x.line[3])
    pairs.append(pairs_of(g_t.line_x))
    g_x.forward((1,))
    g_t.finish()
    pairs.append(pairs_of(g_t.other))
    g_x.forward((2,))
    pairs = jnp.concatenate(pairs, axis=0)
    scores = matmul_nt(enc_q, pairs[:, :enc_width])
    _, powers, total = softmax_part(scores, (enc_width // EH) ** (-0.5) * LOG2E)
    mix = gather_heads(matmul(powers, pairs[:, enc_width:]) / total, EH)
    loads[2].wait()
    latent = (tokens[...].astype(F32) + matmul(mix, w_eo[...])).astype(BF)
    latent_out[...] = latent
    loads[3].wait()
    eb[me] = matmul(normalize(latent), w_emb[...]).astype(BF)
    g_e.start()

    g_x.forward((3,))
    g_e.forward()
    g_e.forward_x()
    g_x.forward_x()
    g_x.finish()
    factor = (dec_width // DH) ** (-0.5) * LOG2E
    hid_keys = xb[:, vis:rows, 0:dec_width].reshape(peers * hid, dec_width)
    hid_values = xb[:, vis:rows, dec_width : 2 * dec_width].reshape(peers * hid, dec_width)
    top_hh, pow_hh, sum_hh = softmax_part(matmul_nt(dec_qh, hid_keys), factor)
    acc_hh = matmul(pow_hh, hid_values)

    g_e.finish()
    rank_hi = jnp.concatenate(
        [xb[:, rows : rows + half, 0:128].astype(F32), xb[:, rows : rows + half, 128:256].astype(F32)], axis=1
    ).reshape(visible_count, 128)
    rank_lo = jnp.concatenate(
        [xb[:, rows : rows + half, 256:384].astype(F32), xb[:, rows : rows + half, 384:512].astype(F32)], axis=1
    ).reshape(visible_count, 128)
    rank = rank_hi * 16.0 + rank_lo
    lane = lax.broadcasted_iota(jnp.int32, (visible_count, 128), 1).astype(F32)
    hot = jnp.concatenate(
        [jnp.where(rank == lane + 128.0 * k, 1.0, 0.0).astype(BF) for k in range(visible_count // 128)], axis=1
    )
    width = eb.shape[2]
    picked = matmul(hot, eb[...].reshape(visible_count, width))
    dec_vis = (picked + xb[:, 0:vis, :].reshape(visible_count, width).astype(F32)).astype(BF)
    din[...] = dec_vis.reshape(peers, vis, width)
    pairs_vis = matmul(normalize(dec_vis), w_dec[:, dec_width:]).astype(BF)
    own_vis = din[me]
    dec_qv = spread_heads(matmul(normalize(own_vis), w_dec[:, :dec_width]).astype(BF), DH)
    vis_keys, vis_values = pairs_vis[:, :dec_width], pairs_vis[:, dec_width:]

    def merge(scores, top, total, acc):
        highest = jnp.maximum(top, jnp.max(scores, -1, keepdims=True))
        powers = jnp.exp2((scores - highest) * factor)
        fade = jnp.exp2((top - highest) * factor)
        total = total * fade + jnp.sum(powers, -1, keepdims=True)
        return (acc * fade + matmul(powers.astype(BF), vis_values)) / total

    mix_h = gather_heads(merge(matmul_nt(dec_qh, vis_keys), top_hh, sum_hh, acc_hh), DH)
    top_vh, pow_vh, sum_vh = softmax_part(matmul_nt(dec_qv, hid_keys), factor)
    acc_vh = matmul(pow_vh, hid_values)
    mix_v = gather_heads(merge(matmul_nt(dec_qv, vis_keys), top_vh, sum_vh, acc_vh), DH)

    dec_in = jnp.concatenate([own_vis, dec_hid], axis=0)
    dec_mix = jnp.concatenate([mix_v, mix_h], axis=0)
    loads[4].wait()
    middle = (dec_in.astype(F32) + matmul(dec_mix, w_do[...])).astype(BF)
    loads[5].wait()
    wide = matmul(normalize(middle), w_ex[...])
    hidden = (0.5 * wide * (1.0 + erf(wide * 0.7071067811865476))).astype(BF)
    loads[6].wait()
    decoded = (middle.astype(F32) + matmul(hidden, w_sh[...])).astype(BF)
    decoded_out[...] = matmul(from_slot, decoded).astype(BF)
    g_t.sent()
    g_x.sent()
    g_e.sent()


def on_device(peers, tokens, order, enc_proj, enc_out, embed, mask, pos, dec_proj, dec_out, expand, shrink):
    vis, rows, width = tokens.shape[0], pos.shape[0], pos.shape[1]
    weights = (enc_proj, enc_out, embed, dec_proj, dec_out, expand, shrink)
    vmem = pl.BlockSpec(memory_space=pltpu.VMEM)
    anywhere = pl.BlockSpec(memory_space=pl.ANY)
    return pl.pallas_call(
        kernel,
        out_shape=(
            jax.ShapeDtypeStruct(tokens.shape, BF),
            jax.ShapeDtypeStruct(pos.shape, BF),
        ),
        in_specs=[vmem, vmem, anywhere, anywhere, anywhere, vmem, vmem, anywhere, anywhere, anywhere, anywhere],
        out_specs=(vmem, vmem),
        scratch_shapes=[pltpu.VMEM(w.shape, BF) for w in weights]
        + [
            pltpu.VMEM((peers, vis, tokens.shape[1]), BF),
            pltpu.VMEM((peers, rows + vis // 2, width), BF),
            pltpu.VMEM((peers, vis, width), BF),
            pltpu.VMEM((peers, vis, width), BF),
            pltpu.SemaphoreType.DMA((7,)),
        ]
        + [pltpu.SemaphoreType.DMA((n,)) for _ in range(3) for n in (15, peers)],
        compiler_params=pltpu.CompilerParams(
            collective_id=0, has_side_effects=True, vmem_limit_bytes=56 * 1024 * 1024
        ),
    )(tokens, order.reshape(1, rows), enc_proj, enc_out, embed, mask, pos,
      dec_proj, dec_out, expand, shrink)


def solution(mesh):
    in_specs = (
        P(("groups", "seq"), None),
        P(("groups", "seq")),
        P(),
        P(),
        P(),
        P(),
        P("seq", None),
        P(),
        P(),
        P(),
        P(),
    )
    out_specs = (P(("groups", "seq"), None), P(("groups", "seq"), None))
    peers = mesh.shape["seq"]
    body = functools.partial(on_device, peers) if peers == 16 else on_device_plain
    return jax.shard_map(
        body, mesh=mesh, in_specs=in_specs, out_specs=out_specs, check_vma=False
    )
```
